128 devices in a mesh: blk: 32 (over x, y, core), red: 4 (over z).
Axes of the slice: x: 4, y: 4, z: 4, core: 2. Of those that a mesh axis runs over, the one named last changes fastest.
Arguments:
- amplitudes: bfloat16 [16, 8, 1024, 1024], P('red', None, 'blk'), may hold values from -6 to 6
- dressed: bfloat16 [16, 8, 1024, 1024], P('red', None, 'blk'), may hold values from -0.125 to 0.125
- integrals: bfloat16 [8, 8, 1024, 1024], P(None, None, 'blk', 'red'), may hold values from -8 to 8
- occ_irrep: int32 [200], replicated, may hold values from 0 to 7
- virt_irrep: int32 [1024], replicated, may hold values from 0 to 7
- occ_energy: float32 [200], replicated, may hold values from -2 to -0.3
- virt_energy: float32 [1024], replicated, may hold values from 0.1 to 4
- slab_i: int32 [8], replicated, may hold values from 0 to 199
- slab_j: int32 [8], replicated, may hold values from 0 to 199
- slab_k: int32 [16], P('red'), may hold values from 0 to 199
Outputs:
- updated: float32 [8, 8, 1024, 1024], P(None, None, 'blk', 'red')
The draws below stay inside these ranges and needn't reach their ends.
Inputs may be any that keep to these rules, and one draw needn't show every extreme that they name: `occ_irrep`: irrep labels of the eight irreps of D2h. `virt_irrep`: irrep labels of the eight irreps of D2h. `slab_i`: indices into the 200 occupied orbitals, repeats allowed. `slab_j`: indices into the 200 occupied orbitals, repeats allowed. `slab_k`: indices into the 200 occupied orbitals, repeats allowed.
All inputs are finite; a program needn't handle non-finite values.
Results may differ from the reference program's by a relative error of at most 0.0003.
Values may be sent and summed in bfloat16 or wider, within the bound.
No kernel may reach another device: no remote copies, remote signals or barrier semaphores. Data moves between devices by JAX's collectives and lax.ppermute only.
A program may use at most 192 MiB of HBM per device.

```python
import jax
import jax.numpy as jnp
from jax import lax

O = 200
V = 1024
I_SL = 8
J_SL = 8
K_SL = 16


def touch_ends(values, own_key, smallest, high):
    spot = [jax.random.randint(jax.random.fold_in(own_key, axis), (), 0, length) for axis, length in enumerate(values.shape)]
    widest = values.shape.index(max(values.shape))
    next_to = spot[:widest] + [(spot[widest] + 1) % values.shape[widest]] + spot[widest + 1:]
    return values.at[tuple(spot)].set(smallest).at[tuple(next_to)].set(high)


def level_of(stream_key, extent, shards, low, largest):
    loudness, own = 1.0, jax.random.fold_in(stream_key, 6)
    for axis_at, parts in shards:
        heights = jnp.exp(jax.random.uniform(jax.random.fold_in(own, axis_at), (parts,), jnp.float32, low / len(shards), largest / len(shards)))
        loudness = loudness * jnp.repeat(heights, extent[axis_at] // parts).reshape([-1 if axis == axis_at else 1 for axis in range(len(extent))])
    return loudness


def bell_draw(rng, shape, deviation, bound, pieces=(), kind=jnp.bfloat16):
    loudness = level_of(rng, shape, pieces, -0.22, 0.18) if pieces else 1.0
    result = jax.random.normal(rng, shape, jnp.float32) * deviation * loudness
    return jnp.minimum(jnp.maximum(result, -bound), bound).astype(kind)


def setup_inputs(seed: int = 0) -> dict:
    seeds = jax.random.split(jax.random.key(seed), 11)
    return {
        "amplitudes": bell_draw(seeds[0], (K_SL, I_SL, V, V), 1.0, 6.0, ((0, 4), (2, 32))),
        "dressed": bell_draw(seeds[1], (K_SL, J_SL, V, V), (K_SL * V // 8) ** -0.5, 0.125, ((0, 4), (2, 32))),
        "integrals": bell_draw(seeds[2], (I_SL, J_SL, V, V), 2.0, 8.0, ((2, 32), (3, 4))),
        "occ_irrep": touch_ends(jax.random.randint(seeds[3], (O,), 0, 8), jax.random.fold_in(seeds[3], 1), 0, 7).astype(jnp.int32),
        "virt_irrep": touch_ends(jax.random.randint(seeds[4], (V,), 0, 8), jax.random.fold_in(seeds[4], 1), 0, 7).astype(jnp.int32),
        "occ_energy": jnp.clip(jax.random.uniform(seeds[5], (O,), jnp.float32, -2.0, -0.3), -2.0, -0.3),
        "virt_energy": jnp.clip(jax.random.uniform(seeds[6], (V,), jnp.float32, 0.1, 4.0), 0.1, 4.0),
        "slab_i": touch_ends(jax.random.randint(seeds[7], (I_SL,), 0, O), jax.random.fold_in(seeds[7], 1), 0, O - 1).astype(jnp.int32),
        "slab_j": touch_ends(jax.random.randint(seeds[8], (J_SL,), 0, O), jax.random.fold_in(seeds[8], 1), 0, O - 1).astype(jnp.int32),
        "slab_k": touch_ends(jax.random.randint(seeds[9], (K_SL,), 0, O), jax.random.fold_in(seeds[9], 1), 0, O - 1).astype(jnp.int32),
    }


def reference(amplitudes, dressed, integrals, occ_irrep, virt_irrep, occ_energy, virt_energy, slab_i, slab_j, slab_k):
    label_i = occ_irrep[slab_i]
    label_j = occ_irrep[slab_j]
    label_k = occ_irrep[slab_k]
    pair_virt = jnp.bitwise_xor(virt_irrep[:, None], virt_irrep[None, :])
    amp_sym = jnp.bitwise_xor(jnp.bitwise_xor(label_k[:, None], label_i[None, :])[:, :, None, None], pair_virt[None, None])
    kept_amp = jnp.where(amp_sym == 0, amplitudes, jnp.zeros((), amplitudes.dtype))
    dre_sym = jnp.bitwise_xor(jnp.bitwise_xor(label_k[:, None], label_j[None, :])[:, :, None, None], pair_virt[None, None])
    kept_dre = jnp.where(dre_sym == 0, dressed, jnp.zeros((), dressed.dtype))
    dressed_wide = kept_dre.astype(jnp.float32)

    def one_slab(amp_row):
        return jnp.einsum('kac,kjcb->jab', amp_row.astype(jnp.float32), dressed_wide)

    cycle = lax.map(one_slab, jnp.moveaxis(kept_amp, 1, 0))
    energy_i = occ_energy[slab_i]
    energy_j = occ_energy[slab_j]
    denom = (energy_i[:, None, None, None] + energy_j[None, :, None, None]) - virt_energy[None, None, :, None] - virt_energy[None, None, None, :]
    out_sym = jnp.bitwise_xor(jnp.bitwise_xor(label_i[:, None], label_j[None, :])[:, :, None, None], pair_virt[None, None])
    value = (integrals.astype(jnp.float32) + cycle) / denom
    return jnp.where(out_sym == 0, value, jnp.zeros((), jnp.float32))
```

```python
import functools

import jax
import jax.numpy as jnp
import numpy as np
from jax import lax
from jax.experimental import pallas as pl
from jax.experimental.pallas import tpu as pltpu
from jax.sharding import PartitionSpec as P

F32 = jnp.float32
BF16 = jnp.bfloat16
I32 = jnp.int32

RING = 4
CORES = 2
WIDE = 192
PART = 64
NT = (((1,), (1,)), ((), ()))


def table_lookup(table, picks):
    hits = picks[:, None] == jnp.arange(table.shape[0], dtype=jnp.int32)[None, :]
    return jnp.sum(jnp.where(hits, table[None, :], jnp.zeros((), table.dtype)), axis=1)


def dense_form(
    amplitudes,
    dressed,
    integrals,
    occ_irrep,
    virt_irrep,
    occ_energy,
    virt_energy,
    slab_i,
    slab_j,
    slab_k,
):
    blk_size = lax.axis_size("blk")
    red_size = lax.axis_size("red")
    k_local, slab_rows, virt_rows, virt_all = amplitudes.shape
    occ_cols = dressed.shape[1]
    cols_kept = virt_all // red_size
    pair_count = slab_rows * occ_cols // blk_size
    own_rows = max(1, pair_count // occ_cols)
    own_cols = min(pair_count, occ_cols)
    owners = np.arange(blk_size)
    first_pair = owners * pair_count
    table_rows = ((first_pair // occ_cols)[:, None] + np.arange(own_rows)[None, :]).reshape(-1)
    table_cols = ((first_pair % occ_cols)[:, None] + np.arange(own_cols)[None, :]).reshape(-1)
    blk_place = lax.axis_index("blk")
    red_place = lax.axis_index("red")
    label_i = table_lookup(occ_irrep, slab_i)
    label_j = table_lookup(occ_irrep, slab_j)
    label_k = table_lookup(occ_irrep, slab_k)
    rows_label = lax.dynamic_slice_in_dim(virt_irrep, blk_place * virt_rows, virt_rows)
    pair_virt = jnp.bitwise_xor(rows_label[:, None], virt_irrep[None, :])
    amp_sym = jnp.bitwise_xor(
        jnp.bitwise_xor(label_k[:, None], label_i[None, :])[:, :, None, None], pair_virt[None, None]
    )
    kept_amp = jnp.where(amp_sym == 0, amplitudes, jnp.zeros((), amplitudes.dtype))
    dre_sym = jnp.bitwise_xor(
        jnp.bitwise_xor(label_k[:, None], label_j[None, :])[:, :, None, None], pair_virt[None, None]
    )
    kept_dre = jnp.where(dre_sym == 0, dressed, jnp.zeros((), dressed.dtype))
    send_amp = jnp.take(kept_amp, table_rows, axis=1).reshape(
        k_local, blk_size, own_rows, virt_rows, virt_all
    )
    send_dre = jnp.take(kept_dre, table_cols, axis=1).reshape(
        k_local, blk_size, own_cols, virt_rows, virt_all
    )
    amp_owner = lax.all_to_all(send_amp, "blk", split_axis=1, concat_axis=3, tiled=True)[:, 0]
    dre_owner = lax.all_to_all(send_dre, "blk", split_axis=1, concat_axis=3, tiled=True)[:, 0]
    partial_cycle = jnp.einsum(
        "kiac,kjcb->ijab", amp_owner, dre_owner, preferred_element_type=jnp.float32
    )
    summed = lax.psum_scatter(partial_cycle, "red", scatter_dimension=3, tiled=True)
    cycle_pairs = summed.reshape(pair_count, virt_all, cols_kept)
    cycle_kept = lax.all_to_all(
        cycle_pairs, "blk", split_axis=1, concat_axis=0, tiled=True
    ).reshape(slab_rows, occ_cols, virt_rows, cols_kept)
    energy_i = table_lookup(occ_energy, slab_i)
    energy_j = table_lookup(occ_energy, slab_j)
    energy_a = lax.dynamic_slice_in_dim(virt_energy, blk_place * virt_rows, virt_rows)
    energy_b = lax.dynamic_slice_in_dim(virt_energy, red_place * cols_kept, cols_kept)
    label_b = lax.dynamic_slice_in_dim(virt_irrep, red_place * cols_kept, cols_kept)
    denom = (
        energy_i[:, None, None, None]
        + energy_j[None, :, None, None]
        - energy_a[None, None, :, None]
        - energy_b[None, None, None, :]
    )
    out_virt = jnp.bitwise_xor(rows_label[:, None], label_b[None, :])
    out_sym = jnp.bitwise_xor(
        jnp.bitwise_xor(label_i[:, None], label_j[None, :])[:, :, None, None], out_virt[None, None]
    )
    value = (integrals.astype(jnp.float32) + cycle_kept) / denom
    return jnp.where(out_sym == 0, value, jnp.zeros((), jnp.float32))


def coords():
    blk = lax.axis_index("blk")
    return blk // (RING * CORES), (blk // CORES) % RING, blk % CORES, lax.axis_index("red")


def iota(shape, dim):
    return lax.broadcasted_iota(I32, shape, dim)


def picked_column(row, first, count):
    wide = row.shape[1]
    hit = iota((count, wide), 1) == iota((count, wide), 0) + first
    kept = jnp.where(hit, jnp.broadcast_to(row.astype(F32), (count, wide)), 0.0)
    return jnp.sum(kept, axis=1, keepdims=True).astype(row.dtype)


def rank_kernel(lv_ref, rank_ref, part_ref, fits_ref):
    wide = lv_ref.shape[1]
    quarter = wide // RING
    tri = (iota((quarter, quarter), 0) < iota((quarter, quarter), 1)).astype(F32).astype(BF16)
    base = jnp.zeros((16, 1), F32)
    most_part = jnp.zeros((1, 1), F32)
    for part in range(RING):
        lanes = slice(part * quarter, (part + 1) * quarter)
        member = (iota((16, quarter), 0) == lv_ref[:, lanes]).astype(F32)
        before = jnp.dot(member.astype(BF16), tri, preferred_element_type=F32)
        part_ref[:, lanes] = jnp.sum(member * before, axis=0, keepdims=True).astype(I32)
        rank_ref[:, lanes] = jnp.sum(member * (before + base), axis=0, keepdims=True).astype(I32)
        count = jnp.sum(member, axis=1, keepdims=True)
        most_part = jnp.maximum(most_part, jnp.max(count))
        base = base + count
    fits = jnp.logical_and(jnp.max(base) <= WIDE, jnp.max(most_part) <= PART)
    fits_ref[0] = fits.astype(I32)


def pack_kernel(
    occ_ref,
    si_ref,
    sj_ref,
    sk_ref,
    lv_ref,
    rank_ref,
    part_ref,
    amp_ref,
    dre_ref,
    pa_ref,
    pb0_ref,
    pb1_ref,
    pb2_ref,
    pb3_ref,
    hot_main,
    hot_low,
    hot_high,
    hot_part,
    own_label,
    kept,
):
    _, y, _, z = coords()
    k = pl.program_id(0)
    rows, wide = amp_ref.shape[2:]
    half = hot_main.shape[0]

    @pl.when(k == 0)
    def _():
        rank = rank_ref[...]
        slot = iota((half, wide), 0)
        hot_main[...] = (slot == rank).astype(F32).astype(BF16)
        hot_low[...] = jnp.logical_and(slot + half == rank, slot < PART).astype(F32).astype(BF16)
        hot_high[...] = (
            jnp.logical_and(slot + half - PART == rank, slot >= PART).astype(F32).astype(BF16)
        )
        step = (iota((1, wide), 1) // (wide // RING) - z + RING) % RING
        hot_part[...] = (
            (iota((RING * PART, wide), 0) == step * PART + part_ref[...]).astype(F32).astype(BF16)
        )
        own_label[...] = picked_column(lv_ref[...], lax.axis_index("blk") * rows, rows)

    lv = lv_ref[...]
    lk = occ_ref[sk_ref[k]]

    def put(at, label, block):
        keep = jnp.bitwise_xor(own_label[...], jnp.bitwise_xor(lk, label)) == lv
        kept[at * rows : (at + 1) * rows, :] = jnp.where(keep, block.astype(F32), 0.0).astype(BF16)

    n_i = amp_ref.shape[1]
    for i in range(n_i):
        put(i, occ_ref[si_ref[i]], amp_ref[0, i])
    main = lax.dot_general(kept[...], hot_main[...], NT, preferred_element_type=F32)
    pa_ref[0, :n_i] = main.astype(BF16).reshape(n_i, rows, half)
    lower = n_i * rows // 2
    rest = lax.dot_general(kept[:lower], hot_low[...], NT, preferred_element_type=F32)
    rest += lax.dot_general(kept[lower:], hot_high[...], NT, preferred_element_type=F32)
    pa_ref[0, n_i:] = rest.astype(BF16).reshape(n_i // 2, rows, half)

    for d in range(RING):
        for jj in range(CORES):
            j = ((y + d) % RING) * CORES + jj
            put(jj * RING + d, occ_ref[sj_ref[j]], dre_ref[0, j])
    packed = lax.dot_general(kept[...], hot_part[...], NT, preferred_element_type=F32)
    for d, out in enumerate((pb0_ref, pb1_ref, pb2_ref, pb3_ref)):
        even = packed[d * rows : (d + 1) * rows]
        odd = packed[(RING + d) * rows : (RING + d + 1) * rows]
        pieces = []
        for s in range(RING):
            pieces += [even[:, s * PART : (s + 1) * PART], odd[:, s * PART : (s + 1) * PART]]
        out[0] = jnp.concatenate(pieces, axis=1).astype(BF16)


def unpack_kernel(
    occ_ref, si_ref, sk_ref, lv_ref, rank_ref, p0, p1, p2, p3, out_ref, hot_low, hot_high, order, labels
):
    x, y, core, _ = coords()
    k = pl.program_id(0)
    n_rest, rows, half = p0.shape[1:]
    n_i = n_rest * 2 // 3
    wide = lv_ref.shape[1]

    @pl.when(k == 0)
    def _():
        p = iota((1, wide), 1)
        source = (
            ((x - (p // 128) % RING + RING) % RING) * (rows * 8)
            + ((y - (p // rows) % RING + RING) % RING) * (rows * 2)
            + jnp.bitwise_xor(core, p // (wide // 2)) * rows
            + p % rows
        )
        pick = (iota((wide, wide), 0) == source).astype(F32).astype(BF16)
        which = iota((16, wide), 0)
        both = jnp.where(
            which == 0,
            jnp.broadcast_to(lv_ref[...], (16, wide)),
            jnp.broadcast_to(jnp.minimum(rank_ref[...], 255), (16, wide)),
        )
        moved = jnp.dot(both.astype(F32).astype(BF16), pick, preferred_element_type=F32).astype(I32)
        order[...] = moved[0:1]
        rank = moved[1:2]
        slot = iota((half, wide), 0)
        main = (slot == rank).astype(F32).astype(BF16)
        hot_low[:half] = main
        hot_high[:half] = main
        hot_low[half:] = jnp.logical_and(slot + half == rank, slot < PART).astype(F32).astype(BF16)
        hot_high[half:] = (
            jnp.logical_and(slot + half - PART == rank, slot >= PART).astype(F32).astype(BF16)
        )
        for d in range(RING):
            first = x * (rows * 8) + ((y - d + RING) % RING) * (rows * 2) + core * rows
            labels[d] = picked_column(lv_ref[...], first, rows)

    lk = occ_ref[sk_ref[k]]
    group = n_i // 2
    for d, block in enumerate((p0, p1, p2, p3)):
        rest = block[0, n_i:].reshape(group * rows, half)
        for side, hot in enumerate((hot_low, hot_high)):
            main = block[0, side * group : (side + 1) * group].reshape(group * rows, half)
            spread = jnp.dot(
                jnp.concatenate([main, rest], axis=1), hot[...], preferred_element_type=F32
            )
            for g in range(group):
                i = side * group + g
                label = jnp.bitwise_xor(lk, occ_ref[si_ref[i]])
                keep = jnp.bitwise_xor(labels[d], label) == order[...]
                at = (d * n_i + i) * rows
                out_ref[0, at : at + rows, :] = jnp.where(
                    keep, spread[g * rows : (g + 1) * rows], 0.0
                ).astype(BF16)


def cycle_kernel(a_ref, b0, b1, b2, b3, b4, b5, b6, b7, o0, o1, o2, o3, b_all, total):
    k = pl.program_id(0)
    depth = b0.shape[0] * b0.shape[2]
    for n, b in enumerate((b0, b1, b2, b3, b4, b5, b6, b7)):
        b_all[n * depth : (n + 1) * depth, :] = b[:, 0].reshape(depth, b.shape[3])
    rows = a_ref.shape[1]
    step = rows // 4
    lanes = o0.shape[1]
    for r in range(4):
        at = slice(r * step, (r + 1) * step)
        term = jnp.dot(a_ref[0, at], b_all[...], preferred_element_type=F32)

        @pl.when(k == 0)
        def _():
            total[at] = term

        @pl.when(jnp.logical_and(k > 0, k < pl.num_programs(0) - 1))
        def _():
            total[at] += term

        @pl.when(k == pl.num_programs(0) - 1)
        def _():
            full = total[at] + term
            for d, out in enumerate((o0, o1, o2, o3)):
                out[at] = full[:, d * lanes : (d + 1) * lanes]


def sum_kernel(o0, o1, o2, o3, s0, s1, s2, s3):
    rows = s0.shape[0] * s0.shape[1]
    for d, out in enumerate((s0, s1, s2, s3)):
        at = slice(d * rows, (d + 1) * rows)
        full = ((o0[at] + o1[at]) + o2[at]) + o3[at]
        out[...] = full.reshape(out.shape)


def update_kernel(
    occ_ref,
    si_ref,
    sj_ref,
    oe_ref,
    lv_ref,
    ve_ref,
    part_ref,
    t0,
    t1,
    t2,
    t3,
    int_ref,
    out_ref,
    hot,
    own_label,
    own_energy,
):
    _, y, _, z = coords()
    i = pl.program_id(0)
    rows, lanes = t0.shape[1:]
    kept = int_ref.shape[3]
    cols = pl.ds(pl.multiple_of(z * kept, kept), kept)

    @pl.when(i == 0)
    def _():
        slot = iota((lanes, kept), 0)
        part = part_ref[:, cols]
        for jj in range(CORES):
            hot[:, jj * kept : (jj + 1) * kept] = (
                (slot == part + jj * PART).astype(F32).astype(BF16)
            )
        first = lax.axis_index("blk") * rows
        own_label[...] = picked_column(lv_ref[...], first, rows)
        own_energy[...] = picked_column(ve_ref[...], first, rows)

    x = jnp.concatenate([t[0] for t in (t0, t1, t2, t3)], axis=0)
    top = x.astype(BF16)
    left = x - top.astype(F32)
    mid = left.astype(BF16)
    low = (left - mid.astype(F32)).astype(BF16)
    count = RING * rows
    three = jnp.dot(
        jnp.concatenate([top, mid, low], axis=0), hot[...], preferred_element_type=F32
    )
    cycle = (three[:count] + three[count : 2 * count]) + three[2 * count :]
    label_i = occ_ref[si_ref[i]]
    energy_i = oe_ref[si_ref[i]]
    label_b = lv_ref[:, cols]
    energy_b = ve_ref[:, cols]
    for d in range(RING):
        for jj in range(CORES):
            j = ((y + d) % RING) * CORES + jj
            label = jnp.bitwise_xor(label_i, occ_ref[sj_ref[j]])
            denom = ((energy_i + oe_ref[sj_ref[j]]) - own_energy[...]) - energy_b
            term = cycle[d * rows : (d + 1) * rows, jj * kept : (jj + 1) * kept]
            value = (int_ref[0, j].astype(F32) + term) / denom
            keep = jnp.bitwise_xor(own_label[...], label) == label_b
            out_ref[0, j] = jnp.where(keep, value, 0.0)


SMEM = pl.BlockSpec(memory_space=pltpu.SMEM)


def whole(shape):
    return pl.BlockSpec(shape, lambda n: (0,) * len(shape))


def cost(flops, moved):
    return pl.CostEstimate(flops=flops, bytes_accessed=moved, transcendentals=0)


def ranks(lv):
    wide = lv.shape[1]
    row = jax.ShapeDtypeStruct((1, wide), I32)
    return pl.pallas_call(
        rank_kernel,
        out_shape=(row, row, jax.ShapeDtypeStruct((1,), I32)),
        in_specs=[pl.BlockSpec(memory_space=pltpu.VMEM)],
        out_specs=(
            pl.BlockSpec(memory_space=pltpu.VMEM),
            pl.BlockSpec(memory_space=pltpu.VMEM),
            SMEM,
        ),
        name="ranks",
    )(lv)


def ring_x(d):
    return [
        (8 * x + m, 8 * ((x + d) % RING) + m) for x in range(RING) for m in range(RING * CORES)
    ]


def ring_y(d):
    return [
        (8 * x + 2 * y + c, 8 * x + 2 * ((y + d) % RING) + c)
        for x in range(RING)
        for y in range(RING)
        for c in range(CORES)
    ]


def ring_z(d):
    return [(z, (z + d) % RING) for z in range(RING)]


def other_core():
    return [(b, b ^ 1) for b in range(RING * RING * CORES)]


def packed_form(
    rank,
    part,
    amplitudes,
    dressed,
    integrals,
    occ_irrep,
    virt_irrep,
    occ_energy,
    virt_energy,
    slab_i,
    slab_j,
    slab_k,
):
    n_k, n_i, rows, wide = amplitudes.shape
    n_j = dressed.shape[1]
    kept = integrals.shape[3]
    half = 128
    n_rest = n_i + n_i // 2
    n_cols = RING * CORES * PART
    lv = virt_irrep.reshape(1, wide)
    ve = virt_energy.reshape(1, wide)
    row_spec = whole((1, wide))
    params = pltpu.CompilerParams(vmem_limit_bytes=48 * 1024 * 1024)

    pa, *pb = pl.pallas_call(
        pack_kernel,
        grid=(n_k,),
        out_shape=[jax.ShapeDtypeStruct((n_k, n_rest, rows, half), BF16)]
        + [jax.ShapeDtypeStruct((n_k, rows, n_cols), BF16)] * RING,
        in_specs=[SMEM] * 4
        + [row_spec] * 3
        + [pl.BlockSpec((1, n_i, rows, wide), lambda k: (k, 0, 0, 0))] * 2,
        out_specs=[pl.BlockSpec((1, n_rest, rows, half), lambda k: (k, 0, 0, 0))]
        + [pl.BlockSpec((1, rows, n_cols), lambda k: (k, 0, 0))] * RING,
        scratch_shapes=[
            pltpu.VMEM((half, wide), BF16),
            pltpu.VMEM((half, wide), BF16),
            pltpu.VMEM((half, wide), BF16),
            pltpu.VMEM((RING * PART, wide), BF16),
            pltpu.VMEM((rows, 1), I32),
            pltpu.VMEM((n_i * rows, wide), BF16),
        ],
        compiler_params=params,
        cost_estimate=cost(2 * 2 * n_k * n_i * rows * wide * 256, 5 << 20),
        name="pack",
    )(occ_irrep, slab_i, slab_j, slab_k, lv, rank, part, amplitudes, dressed)

    pb_y = [pb[0]] + [lax.ppermute(pb[d], "blk", ring_y(d)) for d in (1, 3, 2)]
    pb_y = [pb_y[0], pb_y[1], pb_y[3], pb_y[2]]
    mine = jnp.stack(pb_y)
    pa_y = [pa] + [lax.ppermute(pa, "blk", ring_y(d)) for d in (1, 2, 3)]
    across = [mine] + [lax.ppermute(mine, "blk", ring_x(d)) for d in (1, 2, 3)]
    twin = [lax.ppermute(b, "blk", other_core()) for b in across]

    m_rows = RING * n_i * rows
    spread = pl.pallas_call(
        unpack_kernel,
        grid=(n_k,),
        out_shape=jax.ShapeDtypeStruct((n_k, m_rows, wide), BF16),
        in_specs=[SMEM] * 3
        + [row_spec] * 2
        + [pl.BlockSpec((1, n_rest, rows, half), lambda k: (k, 0, 0, 0))] * RING,
        out_specs=pl.BlockSpec((1, m_rows, wide), lambda k: (k, 0, 0)),
        scratch_shapes=[
            pltpu.VMEM((2 * half, wide), BF16),
            pltpu.VMEM((2 * half, wide), BF16),
            pltpu.VMEM((1, wide), I32),
            pltpu.VMEM((RING, rows, 1), I32),
        ],
        compiler_params=params,
        cost_estimate=cost(2 * n_k * m_rows * wide * 256, 10 << 20),
        name="unpack",
    )(occ_irrep, slab_i, slab_k, lv, rank, *pa_y)

    parts = pl.pallas_call(
        cycle_kernel,
        grid=(n_k,),
        out_shape=[jax.ShapeDtypeStruct((m_rows, CORES * PART), F32)] * RING,
        in_specs=[pl.BlockSpec((1, m_rows, wide), lambda k: (k, 0, 0))]
        + [pl.BlockSpec((RING, 1, rows, n_cols), lambda k: (0, k, 0, 0))] * 8,
        out_specs=[pl.BlockSpec((m_rows, CORES * PART), lambda k: (0, 0))] * RING,
        scratch_shapes=[pltpu.VMEM((wide, n_cols), BF16), pltpu.VMEM((m_rows, n_cols), F32)],
        compiler_params=params,
        cost_estimate=cost(2 * n_k * m_rows * wide * n_cols, 14 << 20),
        name="cycle",
    )(spread, *across, *twin)

    sums = [parts[0]] + [lax.ppermute(parts[d], "red", ring_z(d)) for d in (1, 2, 3)]
    terms = pl.pallas_call(
        sum_kernel,
        out_shape=[jax.ShapeDtypeStruct((n_i, rows, CORES * PART), F32)] * RING,
        in_specs=[pl.BlockSpec(memory_space=pltpu.VMEM)] * RING,
        out_specs=[pl.BlockSpec(memory_space=pltpu.VMEM)] * RING,
        cost_estimate=cost(m_rows * 512, 3 << 20),
        name="sums",
    )(*sums)
    back = [terms[0]] + [lax.ppermute(terms[d], "blk", ring_y(RING - d)) for d in (1, 2, 3)]

    return pl.pallas_call(
        update_kernel,
        grid=(n_i,),
        out_shape=jax.ShapeDtypeStruct(integrals.shape, F32),
        in_specs=[SMEM] * 4
        + [row_spec] * 3
        + [pl.BlockSpec((1, rows, CORES * PART), lambda i: (i, 0, 0))] * RING
        + [pl.BlockSpec((1, n_j, rows, kept), lambda i: (i, 0, 0, 0))],
        out_specs=pl.BlockSpec((1, n_j, rows, kept), lambda i: (i, 0, 0, 0)),
        scratch_shapes=[
            pltpu.VMEM((CORES * PART, CORES * kept), BF16),
            pltpu.VMEM((rows, 1), I32),
            pltpu.VMEM((rows, 1), F32),
        ],
        compiler_params=params,
        cost_estimate=cost(2 * 3 * m_rows * 128 * 512, 4 << 20),
        name="update",
    )(occ_irrep, slab_i, slab_j, occ_energy, lv, ve, part, *back, integrals)


def on_device(*args):
    virt_irrep = args[4]
    rank, part, fits = ranks(virt_irrep.reshape(1, -1))
    return lax.cond(
        fits[0] == 1,
        lambda r, p, *a: packed_form(r, p, *a),
        lambda r, p, *a: dense_form(*a),
        rank,
        part,
        *args,
    )


def solution(mesh):
    in_specs = (
        P("red", None, "blk", None),
        P("red", None, "blk", None),
        P(None, None, "blk", "red"),
        P(),
        P(),
        P(),
        P(),
        P(),
        P(),
        P("red"),
    )
    out_specs = P(None, None, "blk", "red")
    return jax.shard_map(
        on_device, mesh=mesh, in_specs=in_specs, out_specs=out_specs, check_vma=False
    )
```

```python
import functools

import jax
import jax.numpy as jnp
import numpy as np
from jax import lax
from jax.experimental import pallas as pl
from jax.experimental.pallas import tpu as pltpu
from jax.sharding import PartitionSpec as P

F32 = jnp.float32
BF16 = jnp.bfloat16
I32 = jnp.int32

RING = 4
CORES = 2
WIDE = 192
PART = 64
NT = (((1,), (1,)), ((), ()))
STEPS = ((2, 1), (3, 0))
CHUNKS = 2


def table_lookup(table, picks):
    hits = picks[:, None] == jnp.arange(table.shape[0], dtype=jnp.int32)[None, :]
    return jnp.sum(jnp.where(hits, table[None, :], jnp.zeros((), table.dtype)), axis=1)


def dense_form(
    amplitudes,
    dressed,
    integrals,
    occ_irrep,
    virt_irrep,
    occ_energy,
    virt_energy,
    slab_i,
    slab_j,
    slab_k,
):
    blk_size = lax.axis_size("blk")
    red_size = lax.axis_size("red")
    k_local, slab_rows, virt_rows, virt_all = amplitudes.shape
    occ_cols = dressed.shape[1]
    cols_kept = virt_all // red_size
    pair_count = slab_rows * occ_cols // blk_size
    own_rows = max(1, pair_count // occ_cols)
    own_cols = min(pair_count, occ_cols)
    owners = np.arange(blk_size)
    first_pair = owners * pair_count
    table_rows = ((first_pair // occ_cols)[:, None] + np.arange(own_rows)[None, :]).reshape(-1)
    table_cols = ((first_pair % occ_cols)[:, None] + np.arange(own_cols)[None, :]).reshape(-1)
    blk_place = lax.axis_index("blk")
    red_place = lax.axis_index("red")
    label_i = table_lookup(occ_irrep, slab_i)
    label_j = table_lookup(occ_irrep, slab_j)
    label_k = table_lookup(occ_irrep, slab_k)
    rows_label = lax.dynamic_slice_in_dim(virt_irrep, blk_place * virt_rows, virt_rows)
    pair_virt = jnp.bitwise_xor(rows_label[:, None], virt_irrep[None, :])
    amp_sym = jnp.bitwise_xor(
        jnp.bitwise_xor(label_k[:, None], label_i[None, :])[:, :, None, None], pair_virt[None, None]
    )
    kept_amp = jnp.where(amp_sym == 0, amplitudes, jnp.zeros((), amplitudes.dtype))
    dre_sym = jnp.bitwise_xor(
        jnp.bitwise_xor(label_k[:, None], label_j[None, :])[:, :, None, None], pair_virt[None, None]
    )
    kept_dre = jnp.where(dre_sym == 0, dressed, jnp.zeros((), dressed.dtype))
    send_amp = jnp.take(kept_amp, table_rows, axis=1).reshape(
        k_local, blk_size, own_rows, virt_rows, virt_all
    )
    send_dre = jnp.take(kept_dre, table_cols, axis=1).reshape(
        k_local, blk_size, own_cols, virt_rows, virt_all
    )
    amp_owner = lax.all_to_all(send_amp, "blk", split_axis=1, concat_axis=3, tiled=True)[:, 0]
    dre_owner = lax.all_to_all(send_dre, "blk", split_axis=1, concat_axis=3, tiled=True)[:, 0]
    partial_cycle = jnp.einsum(
        "kiac,kjcb->ijab", amp_owner, dre_owner, preferred_element_type=jnp.float32
    )
    by_cols = partial_cycle.reshape(pair_count, virt_all, red_size, cols_kept)
    cycle_pairs = lax.all_to_all(by_cols, "red", split_axis=2, concat_axis=2, tiled=True).sum(axis=2)
    cycle_kept = lax.all_to_all(
        cycle_pairs, "blk", split_axis=1, concat_axis=0, tiled=True
    ).reshape(slab_rows, occ_cols, virt_rows, cols_kept)
    energy_i = table_lookup(occ_energy, slab_i)
    energy_j = table_lookup(occ_energy, slab_j)
    energy_a = lax.dynamic_slice_in_dim(virt_energy, blk_place * virt_rows, virt_rows)
    energy_b = lax.dynamic_slice_in_dim(virt_energy, red_place * cols_kept, cols_kept)
    label_b = lax.dynamic_slice_in_dim(virt_irrep, red_place * cols_kept, cols_kept)
    denom = (
        energy_i[:, None, None, None]
        + energy_j[None, :, None, None]
        - energy_a[None, None, :, None]
        - energy_b[None, None, None, :]
    )
    out_virt = jnp.bitwise_xor(rows_label[:, None], label_b[None, :])
    out_sym = jnp.bitwise_xor(
        jnp.bitwise_xor(label_i[:, None], label_j[None, :])[:, :, None, None], out_virt[None, None]
    )
    value = (integrals.astype(jnp.float32) + cycle_kept) / denom
    return jnp.where(out_sym == 0, value, jnp.zeros((), jnp.float32))


def coords():
    blk = lax.axis_index("blk")
    return blk // (RING * CORES), (blk // CORES) % RING, blk % CORES, lax.axis_index("red")


def iota(shape, dim):
    return lax.broadcasted_iota(I32, shape, dim)


def picked_column(row, first, count):
    wide = row.shape[1]
    hit = iota((count, wide), 1) == iota((count, wide), 0) + first
    kept = jnp.where(hit, jnp.broadcast_to(row.astype(F32), (count, wide)), 0.0)
    return jnp.sum(kept, axis=1, keepdims=True).astype(row.dtype)


def one_hot(count, first, row):
    slot = (iota((count, 1), 0) + first).astype(F32).astype(BF16)
    there = jnp.clip(row, -1, 256).astype(F32).astype(BF16)
    return jnp.where(slot == there, jnp.ones((), BF16), jnp.zeros((), BF16))


def rank_kernel(lv_ref, rank_ref, part_ref, fits_ref):
    wide = lv_ref.shape[1]
    quarter = wide // RING
    tri = (iota((quarter, quarter), 0) < iota((quarter, quarter), 1)).astype(F32).astype(BF16)
    base = jnp.zeros((16, 1), F32)
    most_part = jnp.zeros((1, 1), F32)
    for part in range(RING):
        lanes = slice(part * quarter, (part + 1) * quarter)
        member = (iota((16, quarter), 0) == lv_ref[:, lanes]).astype(F32)
        before = jnp.dot(member.astype(BF16), tri, preferred_element_type=F32)
        part_ref[:, lanes] = jnp.sum(member * before, axis=0, keepdims=True).astype(I32)
        rank_ref[:, lanes] = jnp.sum(member * (before + base), axis=0, keepdims=True).astype(I32)
        count = jnp.sum(member, axis=1, keepdims=True)
        most_part = jnp.maximum(most_part, jnp.max(count))
        base = base + count
    fits = jnp.logical_and(jnp.max(base) <= WIDE, jnp.max(most_part) <= PART)
    fits_ref[0] = fits.astype(I32)


def masked_rows(kept, at, label, own_label, lv, block):
    rows = block.shape[0]
    wanted = jnp.bitwise_xor(own_label, label).astype(F32).astype(BF16)
    kept[at * rows : (at + 1) * rows, :] = jnp.where(wanted == lv, block, jnp.zeros((), BF16))


def pack_dressed_kernel(
    occ_ref, sj_ref, sk_ref, lv_ref, part_ref, dre_ref, p0, p1, p2, p3, hot_part, own_label, kept
):
    _, y, _, z = coords()
    k = pl.program_id(0)
    rows, wide = dre_ref.shape[2:]

    @pl.when(k == 0)
    def _():
        step = (iota((1, wide), 1) // (wide // RING) - z + RING) % RING
        hot_part[...] = one_hot(RING * PART, 0, step * PART + jnp.minimum(part_ref[...], PART - 1))
        own_label[...] = picked_column(lv_ref[...], lax.axis_index("blk") * rows, rows)

    lk = occ_ref[sk_ref[k]]
    lv = lv_ref[...].astype(F32).astype(BF16)
    for d in range(RING):
        for jj in range(CORES):
            j = ((y + d) % RING) * CORES + jj
            label = jnp.bitwise_xor(lk, occ_ref[sj_ref[j]])
            masked_rows(kept, jj * RING + d, label, own_label[...], lv, dre_ref[0, j])
    packed = lax.dot_general(kept[...], hot_part[...], NT, preferred_element_type=F32)
    for d, out in enumerate((p0, p1, p2, p3)):
        even = packed[d * rows : (d + 1) * rows]
        odd = packed[(RING + d) * rows : (RING + d + 1) * rows]
        for chunk, steps in enumerate(STEPS):
            pieces = []
            for s in steps:
                pieces += [even[:, s * PART : (s + 1) * PART], odd[:, s * PART : (s + 1) * PART]]
            out[chunk, 0] = jnp.concatenate(pieces, axis=1).astype(BF16)


def pack_amplitudes_kernel(
    occ_ref, si_ref, sk_ref, lv_ref, rank_ref, amp_ref, pa_ref, hot_main, hot_low, hot_high, own_label, kept
):
    k = pl.program_id(0)
    n_i, rows, wide = amp_ref.shape[1:]
    half = hot_main.shape[0]

    @pl.when(k == 0)
    def _():
        rank = rank_ref[...]
        tail = one_hot(half - PART, half, rank)
        empty = jnp.zeros((PART, wide), BF16)
        hot_main[...] = one_hot(half, 0, rank)
        hot_low[:PART] = tail
        hot_low[PART:] = empty
        hot_high[:PART] = empty
        hot_high[PART:] = tail
        own_label[...] = picked_column(lv_ref[...], lax.axis_index("blk") * rows, rows)

    lk = occ_ref[sk_ref[k]]
    lv = lv_ref[...].astype(F32).astype(BF16)
    for i in range(n_i):
        label = jnp.bitwise_xor(lk, occ_ref[si_ref[i]])
        masked_rows(kept, i, label, own_label[...], lv, amp_ref[0, i])
    main = lax.dot_general(kept[...], hot_main[...], NT, preferred_element_type=F32)
    main = main.astype(BF16).reshape(n_i, rows, half)
    lower = n_i * rows // 2
    rest = lax.dot_general(kept[:lower], hot_low[...], NT, preferred_element_type=F32)
    rest += lax.dot_general(kept[lower:], hot_high[...], NT, preferred_element_type=F32)
    rest = rest.astype(BF16).reshape(n_i // 2, rows, half)
    for d in range(RING):
        pa_ref[d, 0, :n_i] = main
        pa_ref[d, 0, n_i:] = rest


def unpack_kernel(
    occ_ref, si_ref, sk_ref, lv_ref, rank_ref, pa_ref, out_ref, hot_low, hot_high, order, labels
):
    x, y, core, _ = coords()
    k = pl.program_id(0)
    n_rest, rows, half = pa_ref.shape[2:]
    n_i = n_rest * 2 // 3
    wide = lv_ref.shape[1]

    @pl.when(k == 0)
    def _():
        p = iota((1, wide), 1)
        source = (
            ((x - (p // 128) % RING + RING) % RING) * (rows * 8)
            + ((y - (p // rows) % RING + RING) % RING) * (rows * 2)
            + jnp.bitwise_xor(core, p // (wide // 2)) * rows
            + p % rows
        )
        pick = (iota((wide, wide), 0) == source).astype(F32).astype(BF16)
        which = iota((16, wide), 0)
        both = jnp.where(
            which == 0,
            jnp.broadcast_to(lv_ref[...], (16, wide)),
            jnp.broadcast_to(jnp.minimum(rank_ref[...], 255), (16, wide)),
        )
        moved = jnp.dot(both.astype(F32).astype(BF16), pick, preferred_element_type=F32).astype(I32)
        order[...] = moved[0:1].astype(F32).astype(BF16)
        rank = moved[1:2]
        main = one_hot(half, 0, rank)
        tail = one_hot(half - PART, half, rank)
        empty = jnp.zeros((PART, wide), BF16)
        hot_low[:half] = main
        hot_high[:half] = main
        hot_low[half : half + PART] = tail
        hot_low[half + PART :] = empty
        hot_high[half : half + PART] = empty
        hot_high[half + PART :] = tail
        for d in range(RING):
            first = x * (rows * 8) + ((y - d + RING) % RING) * (rows * 2) + core * rows
            labels[d] = picked_column(lv_ref[...], first, rows)

    lk = occ_ref[sk_ref[k]]
    group = n_i // 2
    for d in range(RING):
        block = pa_ref.at[(y - d + RING) % RING]
        rest = block[0, n_i:].reshape(group * rows, half)
        for side, hot in enumerate((hot_low, hot_high)):
            main = block[0, side * group : (side + 1) * group].reshape(group * rows, half)
            spread = jnp.dot(
                jnp.concatenate([main, rest], axis=1), hot[...], preferred_element_type=F32
            )
            for g in range(group):
                i = side * group + g
                label = jnp.bitwise_xor(lk, occ_ref[si_ref[i]])
                wanted = jnp.bitwise_xor(labels[d], label).astype(F32).astype(BF16)
                at = (d * n_i + i) * rows
                out_ref[0, at : at + rows, :] = jnp.where(
                    wanted == order[...],
                    spread[g * rows : (g + 1) * rows].astype(BF16),
                    jnp.zeros((), BF16),
                )


def cycle_kernel(a_ref, b0, b1, b2, b3, b4, b5, b6, b7, o0, o1, b_all, total):
    k = pl.program_id(0)
    depth = b0.shape[0] * b0.shape[2]
    for n, b in enumerate((b0, b1, b2, b3, b4, b5, b6, b7)):
        b_all[n * depth : (n + 1) * depth, :] = b[:, 0].reshape(depth, b.shape[3])
    term = jnp.dot(a_ref[0], b_all[...], preferred_element_type=F32)
    lanes = o0.shape[1]

    @pl.when(k == 0)
    def _():
        total[...] = term

    @pl.when(jnp.logical_and(k > 0, k < pl.num_programs(0) - 1))
    def _():
        total[...] += term

    @pl.when(k == pl.num_programs(0) - 1)
    def _():
        full = total[...] + term
        for d, out in enumerate((o0, o1)):
            out[...] = full[:, d * lanes : (d + 1) * lanes]


def sum_kernel(o0, o1, o2, o3, s0, s1, s2, s3):
    for d, out in enumerate((s0, s1, s2, s3)):
        out[...] = ((o0[d] + o1[d]) + o2[d]) + o3[d]


def update_kernel(
    occ_ref,
    si_ref,
    sj_ref,
    oe_ref,
    lv_ref,
    ve_ref,
    part_ref,
    t0,
    t1,
    t2,
    t3,
    int_ref,
    out_ref,
    hot,
    own_label,
    own_energy,
):
    _, y, _, z = coords()
    i = pl.program_id(0)
    rows, lanes = t0.shape[1:]
    kept = int_ref.shape[3]
    cols = pl.ds(pl.multiple_of(z * kept, kept), kept)

    @pl.when(i == 0)
    def _():
        slot = iota((lanes, kept), 0)
        part = part_ref[:, cols]
        for jj in range(CORES):
            one = (slot == part + jj * PART).astype(F32).astype(BF16)
            for n in range(3):
                hot[n * lanes : (n + 1) * lanes, jj * kept : (jj + 1) * kept] = one
        first = lax.axis_index("blk") * rows
        own_label[...] = picked_column(lv_ref[...], first, rows)
        own_energy[...] = picked_column(ve_ref[...], first, rows)

    x = jnp.concatenate([t[0] for t in (t0, t1, t2, t3)], axis=0)
    top = x.astype(BF16)
    left = x - top.astype(F32)
    mid = left.astype(BF16)
    low = (left - mid.astype(F32)).astype(BF16)
    cycle = jnp.dot(
        jnp.concatenate([top, mid, low], axis=1), hot[...], preferred_element_type=F32
    )
    label_i = occ_ref[si_ref[i]]
    energy_i = oe_ref[si_ref[i]]
    label_b = lv_ref[:, cols]
    energy_b = ve_ref[:, cols]
    for d in range(RING):
        for jj in range(CORES):
            j = ((y + d) % RING) * CORES + jj
            label = jnp.bitwise_xor(label_i, occ_ref[sj_ref[j]])
            denom = ((energy_i + oe_ref[sj_ref[j]]) - own_energy[...]) - energy_b
            term = cycle[d * rows : (d + 1) * rows, jj * kept : (jj + 1) * kept]
            value = (int_ref[0, j].astype(F32) + term) / denom
            keep = jnp.bitwise_xor(own_label[...], label) == label_b
            out_ref[0, j] = jnp.where(keep, value, 0.0)


SMEM = pl.BlockSpec(memory_space=pltpu.SMEM)


def whole(shape):
    return pl.BlockSpec(shape, lambda n: (0,) * len(shape))


def cost(flops, moved):
    return pl.CostEstimate(flops=flops, bytes_accessed=moved, transcendentals=0)


def ranks(lv):
    wide = lv.shape[1]
    row = jax.ShapeDtypeStruct((1, wide), I32)
    return pl.pallas_call(
        rank_kernel,
        out_shape=(row, row, jax.ShapeDtypeStruct((1,), I32)),
        in_specs=[pl.BlockSpec(memory_space=pltpu.VMEM)],
        out_specs=(
            pl.BlockSpec(memory_space=pltpu.VMEM),
            pl.BlockSpec(memory_space=pltpu.VMEM),
            SMEM,
        ),
        name="ranks",
    )(lv)


def ring_x(d):
    return [
        (8 * x + m, 8 * ((x + d) % RING) + m) for x in range(RING) for m in range(RING * CORES)
    ]


def ring_y(d):
    return [
        (8 * x + 2 * y + c, 8 * x + 2 * ((y + d) % RING) + c)
        for x in range(RING)
        for y in range(RING)
        for c in range(CORES)
    ]


def groups_y():
    return [
        [8 * x + 2 * y + c for y in range(RING)] for x in range(RING) for c in range(CORES)
    ]


def ring_z(d):
    return [(z, (z + d) % RING) for z in range(RING)]


def other_core():
    return [(b, b ^ 1) for b in range(RING * RING * CORES)]


def packed_form(
    rank,
    part,
    amplitudes,
    dressed,
    integrals,
    occ_irrep,
    virt_irrep,
    occ_energy,
    virt_energy,
    slab_i,
    slab_j,
    slab_k,
):
    n_k, n_i, rows, wide = amplitudes.shape
    n_j = dressed.shape[1]
    kept = integrals.shape[3]
    half = 128
    n_rest = n_i + n_i // 2
    n_cols = RING * CORES * PART // CHUNKS
    lv = virt_irrep.reshape(1, wide)
    ve = virt_energy.reshape(1, wide)
    row_spec = whole((1, wide))
    params = pltpu.CompilerParams(vmem_limit_bytes=32 * 1024 * 1024)

    block = pl.BlockSpec((1, n_i, rows, wide), lambda k: (k, 0, 0, 0))
    pb = pl.pallas_call(
        pack_dressed_kernel,
        grid=(n_k,),
        out_shape=[jax.ShapeDtypeStruct((CHUNKS, n_k, rows, n_cols), BF16)] * RING,
        in_specs=[SMEM] * 3 + [row_spec] * 2 + [block],
        out_specs=[pl.BlockSpec((CHUNKS, 1, rows, n_cols), lambda k: (0, k, 0, 0))] * RING,
        scratch_shapes=[
            pltpu.VMEM((RING * PART, wide), BF16),
            pltpu.VMEM((rows, 1), I32),
            pltpu.VMEM((n_i * rows, wide), BF16),
        ],
        compiler_params=params,
        cost_estimate=cost(2 * n_k * n_i * rows * wide * 256, 10 << 20),
        name="pack_dressed",
    )(occ_irrep, slab_j, slab_k, lv, part, dressed)
    pa = pl.pallas_call(
        pack_amplitudes_kernel,
        grid=(n_k,),
        out_shape=jax.ShapeDtypeStruct((RING, n_k, n_rest, rows, half), BF16),
        in_specs=[SMEM] * 3 + [row_spec] * 2 + [block],
        out_specs=pl.BlockSpec((RING, 1, n_rest, rows, half), lambda k: (0, k, 0, 0, 0)),
        scratch_shapes=[
            pltpu.VMEM((half, wide), BF16),
            pltpu.VMEM((half, wide), BF16),
            pltpu.VMEM((half, wide), BF16),
            pltpu.VMEM((rows, 1), I32),
            pltpu.VMEM((n_i * rows, wide), BF16),
        ],
        compiler_params=params,
        cost_estimate=cost(2 * n_k * n_i * rows * wide * 256, 10 << 20),
        name="pack_amplitudes",
    )(occ_irrep, slab_i, slab_k, lv, rank, amplitudes)

    pb_y = [pb[0]] + [lax.ppermute(pb[d], "blk", ring_y(d)) for d in (1, 2, 3)]
    pa_y = lax.all_to_all(pa, "blk", 0, 0, axis_index_groups=groups_y())

    m_rows = RING * n_i * rows
    spread = pl.pallas_call(
        unpack_kernel,
        grid=(n_k,),
        out_shape=jax.ShapeDtypeStruct((n_k, m_rows, wide), BF16),
        in_specs=[SMEM] * 3
        + [row_spec] * 2
        + [pl.BlockSpec((RING, 1, n_rest, rows, half), lambda k: (0, k, 0, 0, 0))],
        out_specs=pl.BlockSpec((1, m_rows, wide), lambda k: (k, 0, 0)),
        scratch_shapes=[
            pltpu.VMEM((2 * half, wide), BF16),
            pltpu.VMEM((2 * half, wide), BF16),
            pltpu.VMEM((1, wide), BF16),
            pltpu.VMEM((RING, rows, 1), I32),
        ],
        compiler_params=params,
        cost_estimate=cost(2 * n_k * m_rows * wide * 256, 20 << 20),
        name="unpack",
    )(occ_irrep, slab_i, slab_k, lv, rank, pa_y)

    parts = {}
    for chunk, steps in enumerate(STEPS):
        mine = jnp.stack([b[chunk] for b in pb_y])
        if chunk == 0:
            mine, pa = lax.optimization_barrier((mine, pa))
        across = [mine] + [lax.ppermute(mine, "blk", ring_x(d)) for d in (1, 2, 3)]
        if chunk:
            across[1:] = lax.optimization_barrier((across[1:], parts[STEPS[0][0]]))[0]
        twin = [lax.ppermute(b, "blk", other_core()) for b in across]
        parts[steps[0]], parts[steps[1]] = pl.pallas_call(
            cycle_kernel,
            grid=(n_k,),
            out_shape=[jax.ShapeDtypeStruct((m_rows, CORES * PART), F32)] * 2,
            in_specs=[pl.BlockSpec((1, m_rows, wide), lambda k: (k, 0, 0))]
            + [pl.BlockSpec((RING, 1, rows, n_cols), lambda k: (0, k, 0, 0))] * 8,
            out_specs=[pl.BlockSpec((m_rows, CORES * PART), lambda k: (0, 0))] * 2,
            scratch_shapes=[pltpu.VMEM((wide, n_cols), BF16), pltpu.VMEM((m_rows, n_cols), F32)],
            compiler_params=params,
            cost_estimate=cost(2 * n_k * m_rows * wide * n_cols, 14 << 20),
            name="cycle",
        )(spread, *across, *twin)

    sums = [parts[0]] + [lax.ppermute(parts[d], "red", ring_z(d)) for d in (1, 2, 3)]
    lanes = CORES * PART
    terms = pl.pallas_call(
        sum_kernel,
        grid=(2,),
        out_shape=[jax.ShapeDtypeStruct((n_i, rows, lanes), F32)] * RING,
        in_specs=[pl.BlockSpec((RING, n_i // 2, rows, lanes), lambda n: (0, n, 0, 0))] * RING,
        out_specs=[pl.BlockSpec((n_i // 2, rows, lanes), lambda n: (n, 0, 0))] * RING,
        compiler_params=params,
        cost_estimate=cost(m_rows * 512, 3 << 20),
        name="sums",
    )(*[o.reshape(RING, n_i, rows, lanes) for o in sums])
    back = [terms[0]] + [lax.ppermute(terms[d], "blk", ring_y(RING - d)) for d in (1, 2, 3)]

    return pl.pallas_call(
        update_kernel,
        grid=(n_i,),
        out_shape=jax.ShapeDtypeStruct(integrals.shape, F32),
        in_specs=[SMEM] * 4
        + [row_spec] * 3
        + [pl.BlockSpec((1, rows, CORES * PART), lambda i: (i, 0, 0))] * RING
        + [pl.BlockSpec((1, n_j, rows, kept), lambda i: (i, 0, 0, 0))],
        out_specs=pl.BlockSpec((1, n_j, rows, kept), lambda i: (i, 0, 0, 0)),
        scratch_shapes=[
            pltpu.VMEM((3 * CORES * PART, CORES * kept), BF16),
            pltpu.VMEM((rows, 1), I32),
            pltpu.VMEM((rows, 1), F32),
        ],
        compiler_params=params,
        cost_estimate=cost(2 * 3 * m_rows * 128 * 512, 4 << 20),
        name="update",
    )(occ_irrep, slab_i, slab_j, occ_energy, lv, ve, part, *back, integrals)


def on_device(*args):
    virt_irrep = args[4]
    rank, part, fits = ranks(virt_irrep.reshape(1, -1))
    return lax.cond(
        fits[0] == 1,
        lambda r, p, *a: packed_form(r, p, *a),
        lambda r, p, *a: dense_form(*a),
        rank,
        part,
        *args,
    )


def solution(mesh):
    in_specs = (
        P("red", None, "blk", None),
        P("red", None, "blk", None),
        P(None, None, "blk", "red"),
        P(),
        P(),
        P(),
        P(),
        P(),
        P(),
        P("red"),
    )
    out_specs = P(None, None, "blk", "red")
    return jax.shard_map(
        on_device, mesh=mesh, in_specs=in_specs, out_specs=out_specs, check_vma=False
    )
```

```python
import functools

import jax
import jax.numpy as jnp
import numpy as np
from jax import lax
from jax.experimental import pallas as pl
from jax.experimental.pallas import tpu as pltpu
from jax.sharding import PartitionSpec as P

F32 = jnp.float32
BF16 = jnp.bfloat16
I32 = jnp.int32

RING = 4
CORES = 2
WIDE = 192
PARTS = (64, 48)
STEPS = (2, 1, 3, 0)
LANES = 128


def table_lookup(table, picks):
    hits = picks[:, None] == jnp.arange(table.shape[0], dtype=jnp.int32)[None, :]
    return jnp.sum(jnp.where(hits, table[None, :], jnp.zeros((), table.dtype)), axis=1)


def dense_form(
    amplitudes,
    dressed,
    integrals,
    occ_irrep,
    virt_irrep,
    occ_energy,
    virt_energy,
    slab_i,
    slab_j,
    slab_k,
):
    blk_size = lax.axis_size("blk")
    red_size = lax.axis_size("red")
    k_local, slab_rows, virt_rows, virt_all = amplitudes.shape
    occ_cols = dressed.shape[1]
    cols_kept = virt_all // red_size
    pair_count = slab_rows * occ_cols // blk_size
    own_rows = max(1, pair_count // occ_cols)
    own_cols = min(pair_count, occ_cols)
    owners = np.arange(blk_size)
    first_pair = owners * pair_count
    table_rows = ((first_pair // occ_cols)[:, None] + np.arange(own_rows)[None, :]).reshape(-1)
    table_cols = ((first_pair % occ_cols)[:, None] + np.arange(own_cols)[None, :]).reshape(-1)
    blk_place = lax.axis_index("blk")
    red_place = lax.axis_index("red")
    label_i = table_lookup(occ_irrep, slab_i)
    label_j = table_lookup(occ_irrep, slab_j)
    label_k = table_lookup(occ_irrep, slab_k)
    rows_label = lax.dynamic_slice_in_dim(virt_irrep, blk_place * virt_rows, virt_rows)
    pair_virt = jnp.bitwise_xor(rows_label[:, None], virt_irrep[None, :])
    amp_sym = jnp.bitwise_xor(
        jnp.bitwise_xor(label_k[:, None], label_i[None, :])[:, :, None, None], pair_virt[None, None]
    )
    kept_amp = jnp.where(amp_sym == 0, amplitudes, jnp.zeros((), amplitudes.dtype))
    dre_sym = jnp.bitwise_xor(
        jnp.bitwise_xor(label_k[:, None], label_j[None, :])[:, :, None, None], pair_virt[None, None]
    )
    kept_dre = jnp.where(dre_sym == 0, dressed, jnp.zeros((), dressed.dtype))
    send_amp = jnp.take(kept_amp, table_rows, axis=1).reshape(
        k_local, blk_size, own_rows, virt_rows, virt_all
    )
    send_dre = jnp.take(kept_dre, table_cols, axis=1).reshape(
        k_local, blk_size, own_cols, virt_rows, virt_all
    )
    amp_owner = lax.all_to_all(send_amp, "blk", split_axis=1, concat_axis=3, tiled=True)[:, 0]
    dre_owner = lax.all_to_all(send_dre, "blk", split_axis=1, concat_axis=3, tiled=True)[:, 0]
    partial_cycle = jnp.einsum(
        "kiac,kjcb->ijab", amp_owner, dre_owner, preferred_element_type=jnp.float32
    )
    by_cols = partial_cycle.reshape(pair_count, virt_all, red_size, cols_kept)
    cycle_pairs = lax.all_to_all(by_cols, "red", split_axis=2, concat_axis=2, tiled=True).sum(axis=2)
    cycle_kept = lax.all_to_all(
        cycle_pairs, "blk", split_axis=1, concat_axis=0, tiled=True
    ).reshape(slab_rows, occ_cols, virt_rows, cols_kept)
    energy_i = table_lookup(occ_energy, slab_i)
    energy_j = table_lookup(occ_energy, slab_j)
    energy_a = lax.dynamic_slice_in_dim(virt_energy, blk_place * virt_rows, virt_rows)
    energy_b = lax.dynamic_slice_in_dim(virt_energy, red_place * cols_kept, cols_kept)
    label_b = lax.dynamic_slice_in_dim(virt_irrep, red_place * cols_kept, cols_kept)
    denom = (
        energy_i[:, None, None, None]
        + energy_j[None, :, None, None]
        - energy_a[None, None, :, None]
        - energy_b[None, None, None, :]
    )
    out_virt = jnp.bitwise_xor(rows_label[:, None], label_b[None, :])
    out_sym = jnp.bitwise_xor(
        jnp.bitwise_xor(label_i[:, None], label_j[None, :])[:, :, None, None], out_virt[None, None]
    )
    value = (integrals.astype(jnp.float32) + cycle_kept) / denom
    return jnp.where(out_sym == 0, value, jnp.zeros((), jnp.float32))


def coords():
    blk = lax.axis_index("blk")
    return blk // (RING * CORES), (blk // CORES) % RING, blk % CORES, lax.axis_index("red")


def iota(shape, dim):
    return lax.broadcasted_iota(I32, shape, dim)


def picked_column(row, first, count):
    wide = row.shape[1]
    hit = iota((count, wide), 1) == iota((count, wide), 0) + first
    kept = jnp.where(hit, jnp.broadcast_to(row.astype(F32), (count, wide)), 0.0)
    return jnp.sum(kept, axis=1, keepdims=True).astype(row.dtype)


def one_hot(count, first, row):
    slot = (iota((count, 1), 0) + first).astype(F32).astype(BF16)
    there = jnp.clip(row, -1, 256).astype(F32).astype(BF16)
    return jnp.where(slot == there, jnp.ones((), BF16), jnp.zeros((), BF16))


def label_ranks(lv_ref, rank_ref, part_ref, fits_ref):
    wide = lv_ref.shape[1]
    quarter = wide // RING
    tri = (iota((quarter, quarter), 0) < iota((quarter, quarter), 1)).astype(F32).astype(BF16)
    base = jnp.zeros((16, 1), F32)
    most_part = jnp.zeros((1, 1), F32)
    for part in range(RING):
        lanes = slice(part * quarter, (part + 1) * quarter)
        member = (iota((16, quarter), 0) == lv_ref[:, lanes]).astype(F32)
        before = jnp.dot(member.astype(BF16), tri, preferred_element_type=F32)
        part_ref[:, lanes] = jnp.sum(member * before, axis=0, keepdims=True).astype(I32)
        rank_ref[:, lanes] = jnp.sum(member * (before + base), axis=0, keepdims=True).astype(I32)
        count = jnp.sum(member, axis=1, keepdims=True)
        most_part = jnp.maximum(most_part, jnp.max(count))
        base = base + count
    most = jnp.max(most_part)
    fits = jnp.logical_and(jnp.max(base) <= WIDE, most <= PARTS[0])
    tight = jnp.logical_and(fits, most <= PARTS[1])
    fits_ref[0] = fits.astype(I32) + tight.astype(I32)


def masked_rows(kept, at, label, own_label, lv, block):
    rows = block.shape[0]
    wanted = jnp.bitwise_xor(own_label, label).astype(F32).astype(BF16)
    kept[at * rows : (at + 1) * rows, :] = jnp.where(wanted == lv, block, jnp.zeros((), BF16))


def pack_dressed_kernel(
    slots,
    occ_ref,
    sj_ref,
    sk_ref,
    lv_ref,
    dre_ref,
    p0,
    p1,
    p2,
    p3,
    rank_ref,
    part_ref,
    fits_ref,
    hot_part,
    own_label,
    kept,
):
    _, y, _, z = coords()
    n = pl.program_id(0)
    n_k, _, rows, wide = dre_ref.shape
    lv = lv_ref[...].astype(F32).astype(BF16)

    @pl.when(n == 0)
    def _():
        label_ranks(lv_ref, rank_ref, part_ref, fits_ref)
        step = (iota((1, wide), 1) // (wide // RING) - z + RING) % RING
        first = jnp.zeros((1, wide), I32)
        for n_step, s in enumerate(STEPS):
            first = jnp.where(step == s, n_step * slots, first)
        place = first + jnp.minimum(part_ref[...], slots - 1)
        hot_part[...] = one_hot(RING * slots, 0, place).T
        own_label[...] = picked_column(lv_ref[...], lax.axis_index("blk") * rows, rows)

    for k in range(n_k):
        lk = occ_ref[sk_ref[n * n_k + k]]
        for d in range(RING):
            for jj in range(CORES):
                j = ((y + d) % RING) * CORES + jj
                label = jnp.bitwise_xor(lk, occ_ref[sj_ref[j]])
                at = (jj * RING + d) * n_k + k
                masked_rows(kept, at, label, own_label[...], lv, dre_ref[k, j])
    count = n_k * rows
    packed = jnp.dot(kept[...], hot_part[...], preferred_element_type=F32)
    for d, out in enumerate((p0, p1, p2, p3)):
        even = packed[d * count : (d + 1) * count]
        odd = packed[(RING + d) * count : (RING + d + 1) * count]
        pieces = []
        for s in range(RING):
            at = slice(s * slots, (s + 1) * slots)
            pieces += [even[:, at], odd[:, at]]
        out[...] = jnp.concatenate(pieces, axis=1).astype(BF16).reshape(out.shape)


def pack_amplitudes_kernel(
    occ_ref,
    si_ref,
    sk_ref,
    lv_ref,
    rank_ref,
    amp_ref,
    pa_ref,
    hot_main,
    hot_low,
    hot_high,
    own_label,
    kept,
):
    n = pl.program_id(0)
    n_k, n_i, rows, wide = amp_ref.shape
    half = hot_main.shape[1]
    lv = lv_ref[...].astype(F32).astype(BF16)

    @pl.when(n == 0)
    def _():
        rank = rank_ref[...]
        tail = one_hot(WIDE - half, half, rank)
        empty = jnp.zeros((2 * half - WIDE, wide), BF16)
        hot_main[...] = one_hot(half, 0, rank).T
        hot_low[...] = jnp.concatenate([tail, empty], axis=0).T
        hot_high[...] = jnp.concatenate([empty, tail], axis=0).T
        own_label[...] = picked_column(lv_ref[...], lax.axis_index("blk") * rows, rows)

    for i in range(n_i):
        for k in range(n_k):
            label = jnp.bitwise_xor(occ_ref[sk_ref[n * n_k + k]], occ_ref[si_ref[i]])
            masked_rows(kept, i * n_k + k, label, own_label[...], lv, amp_ref[k, i])
    main = jnp.dot(kept[...], hot_main[...], preferred_element_type=F32).astype(BF16)
    lower = n_i * n_k * rows // 2
    rest = jnp.dot(kept[:lower], hot_low[...], preferred_element_type=F32)
    rest += jnp.dot(kept[lower:], hot_high[...], preferred_element_type=F32)
    main = main.reshape(n_i, n_k, rows, half)
    rest = rest.astype(BF16).reshape(n_i // 2, n_k, rows, half)
    for d in range(RING):
        for k in range(n_k):
            pa_ref[d, k, :n_i] = main[:, k]
            pa_ref[d, k, n_i:] = rest[:, k]


def unpack_kernel(
    occ_ref, si_ref, sk_ref, lv_ref, rank_ref, pa_ref, out_ref, hot_low, hot_high, order, labels
):
    x, y, core, _ = coords()
    k = pl.program_id(0)
    n_rest, rows, half = pa_ref.shape[2:]
    n_i = n_rest * 2 // 3
    wide = lv_ref.shape[1]

    @pl.when(k == 0)
    def _():
        p = iota((1, wide), 1)
        source = (
            ((x - (p // (4 * rows)) % RING + RING) % RING) * (rows * 8)
            + ((y - (p // rows) % RING + RING) % RING) * (rows * 2)
            + jnp.bitwise_xor(core, p // (wide // 2)) * rows
            + p % rows
        )
        pick = (iota((wide, wide), 0) == source).astype(F32).astype(BF16)
        which = iota((16, wide), 0)
        both = jnp.where(
            which == 0,
            jnp.broadcast_to(lv_ref[...], (16, wide)),
            jnp.broadcast_to(jnp.minimum(rank_ref[...], 255), (16, wide)),
        )
        moved = jnp.dot(both.astype(F32).astype(BF16), pick, preferred_element_type=F32).astype(I32)
        order[...] = moved[0:1].astype(F32).astype(BF16)
        rank = moved[1:2]
        main = one_hot(half, 0, rank)
        tail = one_hot(WIDE - half, half, rank)
        empty = jnp.zeros((2 * half - WIDE, wide), BF16)
        hot_low[:half] = main
        hot_high[:half] = main
        hot_low[half:WIDE] = tail
        hot_low[WIDE:] = empty
        hot_high[half:WIDE] = empty
        hot_high[WIDE:] = tail
        for d in range(RING):
            first = x * (rows * 8) + ((y - d + RING) % RING) * (rows * 2) + core * rows
            labels[d] = picked_column(lv_ref[...], first, rows)

    lk = occ_ref[sk_ref[k]]
    group = n_i // 2
    for d in range(RING):
        block = pa_ref.at[(y - d + RING) % RING]
        rest = block[0, n_i:].reshape(group * rows, half)
        for side, hot in enumerate((hot_low, hot_high)):
            main = block[0, side * group : (side + 1) * group].reshape(group * rows, half)
            spread = jnp.dot(
                jnp.concatenate([main, rest], axis=1), hot[...], preferred_element_type=F32
            )
            for g in range(group):
                i = side * group + g
                label = jnp.bitwise_xor(lk, occ_ref[si_ref[i]])
                wanted = jnp.bitwise_xor(labels[d], label).astype(F32).astype(BF16)
                at = (d * n_i + i) * rows
                out_ref[0, at : at + rows, :] = jnp.where(
                    wanted == order[...],
                    spread[g * rows : (g + 1) * rows].astype(BF16),
                    jnp.zeros((), BF16),
                )


def folded(value, n_i, rows):
    used = value.shape[1]
    blocks = [value[n * rows : (n + 1) * rows] for n in range(value.shape[0] // rows)]
    if used == LANES:
        return blocks
    hosts = used // (LANES - used)
    held = n_i * hosts // (hosts + 1)
    out = []
    for d in range(len(blocks) // n_i):
        for i in range(held):
            guest = blocks[d * n_i + held + i // hosts]
            at = (i % hosts) * (LANES - used)
            out.append(
                jnp.concatenate([blocks[d * n_i + i], guest[:, at : at + LANES - used]], axis=1)
            )
    return out


def cycle_kernel(
    n_i, slots, first, a_ref, b0, b1, b2, b3, b4, b5, b6, b7, o0, o1, b_all, total
):
    k = pl.program_id(0)
    rows = b0.shape[2]
    depth = b0.shape[0] * rows
    start = first * CORES * slots // LANES * LANES
    for n, b in enumerate((b0, b1, b2, b3, b4, b5, b6, b7)):
        b_all[n * depth : (n + 1) * depth, :] = b[:, 0, :, start : start + 256].reshape(depth, 256)
    term = jnp.dot(a_ref[0], b_all[...], preferred_element_type=F32)

    @pl.when(k == 0)
    def _():
        total[...] = term

    @pl.when(jnp.logical_and(k > 0, k < pl.num_programs(0) - 1))
    def _():
        total[...] += term

    @pl.when(k == pl.num_programs(0) - 1)
    def _():
        full = total[...] + term
        for n, out in enumerate((o0, o1)):
            at = (first + n) * CORES * slots - start
            for m, block in enumerate(folded(full[:, at : at + CORES * slots], n_i, rows)):
                out[m // out.shape[1], m % out.shape[1]] = block


def sum_kernel(o0, o1, o2, o3, s0, s1, s2, s3):
    for d, out in enumerate((s0, s1, s2, s3)):
        out[...] = ((o0[d] + o1[d]) + o2[d]) + o3[d]


def update_kernel(
    slots,
    occ_ref,
    si_ref,
    sj_ref,
    oe_ref,
    lv_ref,
    ve_ref,
    part_ref,
    t0,
    t1,
    t2,
    t3,
    int_ref,
    out_ref,
    hot,
    own_label,
    own_energy,
    three,
):
    _, y, _, z = coords()
    n = pl.program_id(0)
    held, rows, lanes = t0.shape
    n_i, _, _, kept = int_ref.shape
    cols = pl.ds(pl.multiple_of(z * kept, kept), kept)

    @pl.when(n == 0)
    def _():
        slot = iota((lanes, kept), 0)
        part = part_ref[:, cols]
        for jj in range(CORES):
            one = (slot == part + jj * slots).astype(F32).astype(BF16)
            for n in range(3):
                hot[n * lanes : (n + 1) * lanes, jj * kept : (jj + 1) * kept] = one
        first = lax.axis_index("blk") * rows
        own_label[...] = picked_column(lv_ref[...], first, rows)
        own_energy[...] = picked_column(ve_ref[...], first, rows)

    spare = lanes - CORES * slots

    @pl.when(n == 0)
    def _():
        for d, t in enumerate((t0, t1, t2, t3)):
            for i in range(three.shape[0]):
                if i < held:
                    x = t[i]
                else:
                    hosts = CORES * slots // spare
                    first_host = (i - held) * hosts
                    x = jnp.concatenate(
                        [t[first_host + h][:, lanes - spare :] for h in range(hosts)]
                        + [jnp.zeros((rows, spare), F32)],
                        axis=1,
                    )
                top = x.astype(BF16)
                left = x - top.astype(F32)
                mid = left.astype(BF16)
                low = (left - mid.astype(F32)).astype(BF16)
                three[i, d * rows : (d + 1) * rows] = jnp.concatenate([top, mid, low], axis=1)

    label_b = lv_ref[:, cols]
    energy_b = ve_ref[:, cols]
    for e in range(n_i):
        i = n * n_i + e
        cycle = jnp.dot(three[i], hot[...], preferred_element_type=F32)
        label_i = occ_ref[si_ref[i]]
        energy_i = oe_ref[si_ref[i]]
        for d in range(RING):
            for jj in range(CORES):
                j = ((y + d) % RING) * CORES + jj
                label = jnp.bitwise_xor(label_i, occ_ref[sj_ref[j]])
                denom = ((energy_i + oe_ref[sj_ref[j]]) - own_energy[...]) - energy_b
                term = cycle[d * rows : (d + 1) * rows, jj * kept : (jj + 1) * kept]
                value = (int_ref[e, j].astype(F32) + term) / denom
                keep = jnp.bitwise_xor(own_label[...], label) == label_b
                out_ref[e, j] = jnp.where(keep, value, 0.0)


SMEM = pl.BlockSpec(memory_space=pltpu.SMEM)


def whole(shape):
    return pl.BlockSpec(shape, lambda n: (0,) * len(shape))


def cost(flops, moved):
    return pl.CostEstimate(flops=flops, bytes_accessed=moved, transcendentals=0)


def halves(shape, dim):
    block = tuple(size // 2 if at == dim else size for at, size in enumerate(shape))
    return pl.BlockSpec(block, lambda n: tuple(n if at == dim else 0 for at in range(len(shape))))


def pack_dressed(slots, dressed, occ_irrep, virt_irrep, slab_j, slab_k):
    n_k, n_j, rows, wide = dressed.shape
    out = (n_k, rows, RING * CORES * slots)
    row_spec = whole((1, wide))
    row = jax.ShapeDtypeStruct((1, wide), I32)
    *pb, rank, part, fits = pl.pallas_call(
        functools.partial(pack_dressed_kernel, slots),
        grid=(2,),
        out_shape=[jax.ShapeDtypeStruct(out, BF16)] * RING
        + [row, row, jax.ShapeDtypeStruct((1,), I32)],
        in_specs=[SMEM] * 3 + [row_spec, halves(dressed.shape, 0)],
        out_specs=[halves(out, 0)] * RING + [row_spec, row_spec, SMEM],
        scratch_shapes=[
            pltpu.VMEM((wide, RING * slots), BF16),
            pltpu.VMEM((rows, 1), I32),
            pltpu.VMEM((n_k * n_j * rows // 2, wide), BF16),
        ],
        compiler_params=pltpu.CompilerParams(vmem_limit_bytes=32 * 1024 * 1024),
        cost_estimate=cost(2 * n_k * n_j * rows * wide * 256, 10 << 20),
        name="pack_dressed",
    )(occ_irrep, slab_j, slab_k, virt_irrep.reshape(1, wide), dressed)
    return pb, rank, part, fits


def pack_amplitudes(amplitudes, rank, occ_irrep, virt_irrep, slab_i, slab_k):
    n_k, n_i, rows, wide = amplitudes.shape
    half = LANES
    out = (RING, n_k, n_i + n_i // 2, rows, half)
    row_spec = whole((1, wide))
    return pl.pallas_call(
        pack_amplitudes_kernel,
        grid=(2,),
        out_shape=jax.ShapeDtypeStruct(out, BF16),
        in_specs=[SMEM] * 3 + [row_spec, row_spec, halves(amplitudes.shape, 0)],
        out_specs=halves(out, 1),
        scratch_shapes=[
            pltpu.VMEM((wide, half), BF16),
            pltpu.VMEM((wide, half), BF16),
            pltpu.VMEM((wide, half), BF16),
            pltpu.VMEM((rows, 1), I32),
            pltpu.VMEM((n_k * n_i * rows // 2, wide), BF16),
        ],
        compiler_params=pltpu.CompilerParams(vmem_limit_bytes=32 * 1024 * 1024),
        cost_estimate=cost(2 * n_k * n_i * rows * wide * 256, 10 << 20),
        name="pack_amplitudes",
    )(occ_irrep, slab_i, slab_k, virt_irrep.reshape(1, wide), rank, amplitudes)


def ring_y(d):
    return [
        (8 * x + 2 * y + c, 8 * x + 2 * ((y + d) % RING) + c)
        for x in range(RING)
        for y in range(RING)
        for c in range(CORES)
    ]


def groups_y():
    return [
        [8 * x + 2 * y + c for y in range(RING)] for x in range(RING) for c in range(CORES)
    ]


def ring_x(d):
    return [
        (8 * x + m, 8 * ((x + d) % RING) + m) for x in range(RING) for m in range(RING * CORES)
    ]


def ring_z(d):
    return [(z, (z + d) % RING) for z in range(RING)]


def other_core():
    return [(b, b ^ 1) for b in range(RING * RING * CORES)]


def over_y(pb):
    return [pb[0]] + [lax.ppermute(pb[d], "blk", ring_y(d)) for d in (1, 2, 3)]


def packed_form(
    slots,
    pb_y,
    pa,
    rank,
    part,
    amplitudes,
    integrals,
    occ_irrep,
    virt_irrep,
    occ_energy,
    virt_energy,
    slab_i,
    slab_j,
    slab_k,
):
    n_k, n_i, rows, wide = amplitudes.shape
    n_j = integrals.shape[1]
    kept = integrals.shape[3]
    half = 128
    n_rest = n_i + n_i // 2
    n_cols = RING * CORES * slots
    held = n_i * CORES * slots // LANES
    lv = virt_irrep.reshape(1, wide)
    ve = virt_energy.reshape(1, wide)
    row_spec = whole((1, wide))
    params = pltpu.CompilerParams(vmem_limit_bytes=32 * 1024 * 1024)

    pa_y = lax.all_to_all(pa, "blk", 0, 0, axis_index_groups=groups_y())

    m_rows = RING * n_i * rows
    spread = pl.pallas_call(
        unpack_kernel,
        grid=(n_k,),
        out_shape=jax.ShapeDtypeStruct((n_k, m_rows, wide), BF16),
        in_specs=[SMEM] * 3
        + [row_spec] * 2
        + [pl.BlockSpec((RING, 1, n_rest, rows, half), lambda k: (0, k, 0, 0, 0))],
        out_specs=pl.BlockSpec((1, m_rows, wide), lambda k: (k, 0, 0)),
        scratch_shapes=[
            pltpu.VMEM((2 * half, wide), BF16),
            pltpu.VMEM((2 * half, wide), BF16),
            pltpu.VMEM((1, wide), BF16),
            pltpu.VMEM((RING, rows, 1), I32),
        ],
        compiler_params=params,
        cost_estimate=cost(2 * n_k * m_rows * wide * 256, 20 << 20),
        name="unpack",
    )(occ_irrep, slab_i, slab_k, lv, rank, pa_y)

    mine = jnp.stack(pb_y)
    across = [mine] + [lax.ppermute(mine, "blk", ring_x(d)) for d in (1, 2, 3)]
    twin = [lax.ppermute(b, "blk", other_core()) for b in across]
    parts = {}
    for first in (0, 2):
        parts[STEPS[first]], parts[STEPS[first + 1]] = pl.pallas_call(
            functools.partial(cycle_kernel, n_i, slots, first),
            grid=(n_k,),
            out_shape=[jax.ShapeDtypeStruct((RING, held, rows, LANES), F32)] * 2,
            in_specs=[pl.BlockSpec((1, m_rows, wide), lambda k: (k, 0, 0))]
            + [pl.BlockSpec((RING, 1, rows, n_cols), lambda k: (0, k, 0, 0))] * 8,
            out_specs=[whole((RING, held, rows, LANES))] * 2,
            scratch_shapes=[pltpu.VMEM((wide, 256), BF16), pltpu.VMEM((m_rows, 256), F32)],
            compiler_params=params,
            cost_estimate=cost(2 * n_k * m_rows * wide * 256, 14 << 20),
            name="cycle",
        )(spread, *across, *twin)

    sums = [parts[0]] + [lax.ppermute(parts[d], "red", ring_z(d)) for d in (1, 2, 3)]
    terms = pl.pallas_call(
        sum_kernel,
        grid=(2,),
        out_shape=[jax.ShapeDtypeStruct((held, rows, LANES), F32)] * RING,
        in_specs=[pl.BlockSpec((RING, held // 2, rows, LANES), lambda n: (0, n, 0, 0))] * RING,
        out_specs=[pl.BlockSpec((held // 2, rows, LANES), lambda n: (n, 0, 0))] * RING,
        compiler_params=params,
        cost_estimate=cost(m_rows * 512, 3 << 20),
        name="sums",
    )(*sums)
    back = [terms[0]] + [lax.ppermute(terms[d], "blk", ring_y(RING - d)) for d in (1, 2, 3)]

    return pl.pallas_call(
        functools.partial(update_kernel, slots),
        grid=(n_i // 2,),
        out_shape=jax.ShapeDtypeStruct(integrals.shape, F32),
        in_specs=[SMEM] * 4
        + [row_spec] * 3
        + [whole((held, rows, LANES))] * RING
        + [pl.BlockSpec((2, n_j, rows, kept), lambda n: (n, 0, 0, 0))],
        out_specs=pl.BlockSpec((2, n_j, rows, kept), lambda n: (n, 0, 0, 0)),
        scratch_shapes=[
            pltpu.VMEM((3 * LANES, CORES * kept), BF16),
            pltpu.VMEM((rows, 1), I32),
            pltpu.VMEM((rows, 1), F32),
            pltpu.VMEM((n_i, RING * rows, 3 * LANES), BF16),
        ],
        compiler_params=params,
        cost_estimate=cost(2 * 3 * m_rows * 128 * 512, 4 << 20),
        name="update",
    )(occ_irrep, slab_i, slab_j, occ_energy, lv, ve, part, *back, integrals)


def on_device(
    amplitudes,
    dressed,
    integrals,
    occ_irrep,
    virt_irrep,
    occ_energy,
    virt_energy,
    slab_i,
    slab_j,
    slab_k,
):
    pb_y, rank, part, fits = pack_dressed(
        PARTS[1], dressed, occ_irrep, virt_irrep, slab_j, slab_k
    )
    pb_y = over_y(pb_y)
    pa = pack_amplitudes(amplitudes, rank, occ_irrep, virt_irrep, slab_i, slab_k)
    rest = (integrals, occ_irrep, virt_irrep, occ_energy, virt_energy, slab_i, slab_j, slab_k)

    def dense(pb_y, pa, rank, part, fits, a, d, *rest):
        return dense_form(a, d, *rest)

    def loose(pb_y, pa, rank, part, fits, a, d, *rest):
        pb, rank, part, _ = pack_dressed(PARTS[0], d, rest[1], rest[2], rest[6], rest[7])
        return packed_form(PARTS[0], over_y(pb), pa, rank, part, a, *rest)

    def tight(pb_y, pa, rank, part, fits, a, d, *rest):
        return packed_form(PARTS[1], pb_y, pa, rank, part, a, *rest)

    def other(pb_y, pa, rank, part, fits, *arrays):
        return lax.cond(fits[0] == 1, loose, dense, pb_y, pa, rank, part, fits, *arrays)

    return lax.cond(
        fits[0] == 2, tight, other, pb_y, pa, rank, part, fits, amplitudes, dressed, *rest
    )


def solution(mesh):
    in_specs = (
        P("red", None, "blk", None),
        P("red", None, "blk", None),
        P(None, None, "blk", "red"),
        P(),
        P(),
        P(),
        P(),
        P(),
        P(),
        P("red"),
    )
    out_specs = P(None, None, "blk", "red")
    return jax.shard_map(
        on_device, mesh=mesh, in_specs=in_specs, out_specs=out_specs, check_vma=False
    )
```

```python
import functools

import jax
import jax.numpy as jnp
import numpy as np
from jax import lax
from jax.experimental import pallas as pl
from jax.experimental.pallas import tpu as pltpu
from jax.sharding import PartitionSpec as P

F32 = jnp.float32
BF16 = jnp.bfloat16
I32 = jnp.int32

RING = 4
CORES = 2
WIDES = (192, 160)
PARTS = (64, 48)
STEPS = (1, 3, 2, 0)
LANES = 128


def table_lookup(table, picks):
    hits = picks[:, None] == jnp.arange(table.shape[0], dtype=jnp.int32)[None, :]
    return jnp.sum(jnp.where(hits, table[None, :], jnp.zeros((), table.dtype)), axis=1)


def dense_form(
    amplitudes,
    dressed,
    integrals,
    occ_irrep,
    virt_irrep,
    occ_energy,
    virt_energy,
    slab_i,
    slab_j,
    slab_k,
):
    blk_size = lax.axis_size("blk")
    red_size = lax.axis_size("red")
    k_local, slab_rows, virt_rows, virt_all = amplitudes.shape
    occ_cols = dressed.shape[1]
    cols_kept = virt_all // red_size
    pair_count = slab_rows * occ_cols // blk_size
    own_rows = max(1, pair_count // occ_cols)
    own_cols = min(pair_count, occ_cols)
    owners = np.arange(blk_size)
    first_pair = owners * pair_count
    table_rows = ((first_pair // occ_cols)[:, None] + np.arange(own_rows)[None, :]).reshape(-1)
    table_cols = ((first_pair % occ_cols)[:, None] + np.arange(own_cols)[None, :]).reshape(-1)
    blk_place = lax.axis_index("blk")
    red_place = lax.axis_index("red")
    label_i = table_lookup(occ_irrep, slab_i)
    label_j = table_lookup(occ_irrep, slab_j)
    label_k = table_lookup(occ_irrep, slab_k)
    rows_label = lax.dynamic_slice_in_dim(virt_irrep, blk_place * virt_rows, virt_rows)
    pair_virt = jnp.bitwise_xor(rows_label[:, None], virt_irrep[None, :])
    amp_sym = jnp.bitwise_xor(
        jnp.bitwise_xor(label_k[:, None], label_i[None, :])[:, :, None, None], pair_virt[None, None]
    )
    kept_amp = jnp.where(amp_sym == 0, amplitudes, jnp.zeros((), amplitudes.dtype))
    dre_sym = jnp.bitwise_xor(
        jnp.bitwise_xor(label_k[:, None], label_j[None, :])[:, :, None, None], pair_virt[None, None]
    )
    kept_dre = jnp.where(dre_sym == 0, dressed, jnp.zeros((), dressed.dtype))
    send_amp = jnp.take(kept_amp, table_rows, axis=1).reshape(
        k_local, blk_size, own_rows, virt_rows, virt_all
    )
    send_dre = jnp.take(kept_dre, table_cols, axis=1).reshape(
        k_local, blk_size, own_cols, virt_rows, virt_all
    )
    amp_owner = lax.all_to_all(send_amp, "blk", split_axis=1, concat_axis=3, tiled=True)[:, 0]
    dre_owner = lax.all_to_all(send_dre, "blk", split_axis=1, concat_axis=3, tiled=True)[:, 0]
    partial_cycle = jnp.einsum(
        "kiac,kjcb->ijab", amp_owner, dre_owner, preferred_element_type=jnp.float32
    )
    by_cols = partial_cycle.reshape(pair_count, virt_all, red_size, cols_kept)
    cycle_pairs = lax.all_to_all(by_cols, "red", split_axis=2, concat_axis=2, tiled=True).sum(axis=2)
    cycle_kept = lax.all_to_all(
        cycle_pairs, "blk", split_axis=1, concat_axis=0, tiled=True
    ).reshape(slab_rows, occ_cols, virt_rows, cols_kept)
    energy_i = table_lookup(occ_energy, slab_i)
    energy_j = table_lookup(occ_energy, slab_j)
    energy_a = lax.dynamic_slice_in_dim(virt_energy, blk_place * virt_rows, virt_rows)
    energy_b = lax.dynamic_slice_in_dim(virt_energy, red_place * cols_kept, cols_kept)
    label_b = lax.dynamic_slice_in_dim(virt_irrep, red_place * cols_kept, cols_kept)
    denom = (
        energy_i[:, None, None, None]
        + energy_j[None, :, None, None]
        - energy_a[None, None, :, None]
        - energy_b[None, None, None, :]
    )
    out_virt = jnp.bitwise_xor(rows_label[:, None], label_b[None, :])
    out_sym = jnp.bitwise_xor(
        jnp.bitwise_xor(label_i[:, None], label_j[None, :])[:, :, None, None], out_virt[None, None]
    )
    value = (integrals.astype(jnp.float32) + cycle_kept) / denom
    return jnp.where(out_sym == 0, value, jnp.zeros((), jnp.float32))


def coords():
    blk = lax.axis_index("blk")
    return blk // (RING * CORES), (blk // CORES) % RING, blk % CORES, lax.axis_index("red")


def iota(shape, dim):
    return lax.broadcasted_iota(I32, shape, dim)


def picked_column(row, first, count):
    wide = row.shape[1]
    hit = iota((count, wide), 1) == iota((count, wide), 0) + first
    kept = jnp.where(hit, jnp.broadcast_to(row.astype(F32), (count, wide)), 0.0)
    return jnp.sum(kept, axis=1, keepdims=True).astype(row.dtype)


def one_hot(count, first, row):
    slot = (iota((count, 1), 0) + first).astype(F32).astype(BF16)
    there = jnp.clip(row, -1, 256).astype(F32).astype(BF16)
    return jnp.where(slot == there, jnp.ones((), BF16), jnp.zeros((), BF16))


def rest_hot(groups, group, half, rank):
    share = half // groups
    slot = iota((half, 1), 0) - group * share
    inside = jnp.logical_and(slot >= 0, slot < share)
    slot = jnp.where(inside, slot + half, 512).astype(F32).astype(BF16)
    there = jnp.clip(rank, -1, 256).astype(F32).astype(BF16)
    return jnp.where(slot == there, jnp.ones((), BF16), jnp.zeros((), BF16))


def label_ranks(lv_ref, rank_ref, part_ref, fits_ref):
    wide = lv_ref.shape[1]
    quarter = wide // RING
    tri = (iota((quarter, quarter), 0) < iota((quarter, quarter), 1)).astype(F32).astype(BF16)
    base = jnp.zeros((16, 1), F32)
    most_part = jnp.zeros((1, 1), F32)
    for part in range(RING):
        lanes = slice(part * quarter, (part + 1) * quarter)
        member = (iota((16, quarter), 0) == lv_ref[:, lanes]).astype(F32)
        before = jnp.dot(member.astype(BF16), tri, preferred_element_type=F32)
        part_ref[:, lanes] = jnp.sum(member * before, axis=0, keepdims=True).astype(I32)
        rank_ref[:, lanes] = jnp.sum(member * (before + base), axis=0, keepdims=True).astype(I32)
        count = jnp.sum(member, axis=1, keepdims=True)
        most_part = jnp.maximum(most_part, jnp.max(count))
        base = base + count
    most = jnp.max(most_part)
    whole_most = jnp.max(base)
    fits = jnp.logical_and(whole_most <= WIDES[0], most <= PARTS[0])
    tight = jnp.logical_and(whole_most <= WIDES[1], most <= PARTS[1])
    fits_ref[0] = fits.astype(I32) + tight.astype(I32)


def masked_rows(kept, at, label, own_label, lv, block):
    rows = block.shape[0]
    wanted = jnp.bitwise_xor(own_label, label).astype(F32).astype(BF16)
    kept[at * rows : (at + 1) * rows, :] = jnp.where(wanted == lv, block, jnp.zeros((), BF16))


def pack_dressed_kernel(
    slots,
    occ_ref,
    sj_ref,
    sk_ref,
    lv_ref,
    dre_ref,
    p0,
    p1,
    p2,
    p3,
    rank_ref,
    part_ref,
    fits_ref,
    hot_part,
    own_label,
    kept,
):
    _, y, _, z = coords()
    n = pl.program_id(0)
    n_k, _, rows, wide = dre_ref.shape
    lv = lv_ref[...].astype(F32).astype(BF16)

    @pl.when(n == 0)
    def _():
        label_ranks(lv_ref, rank_ref, part_ref, fits_ref)
        step = (iota((1, wide), 1) // (wide // RING) - z + RING) % RING
        first = jnp.zeros((1, wide), I32)
        for n_step, s in enumerate(STEPS):
            first = jnp.where(step == s, n_step * slots, first)
        place = first + jnp.minimum(part_ref[...], slots - 1)
        hot_part[...] = one_hot(RING * slots, 0, place).T
        own_label[...] = picked_column(lv_ref[...], lax.axis_index("blk") * rows, rows)

    for k in range(n_k):
        lk = occ_ref[sk_ref[n * n_k + k]]
        for d in range(RING):
            for jj in range(CORES):
                j = ((y + d) % RING) * CORES + jj
                label = jnp.bitwise_xor(lk, occ_ref[sj_ref[j]])
                at = (jj * RING + d) * n_k + k
                masked_rows(kept, at, label, own_label[...], lv, dre_ref[k, j])
    count = n_k * rows
    packed = jnp.dot(kept[...], hot_part[...], preferred_element_type=F32)
    for d, out in enumerate((p0, p1, p2, p3)):
        even = packed[d * count : (d + 1) * count]
        odd = packed[(RING + d) * count : (RING + d + 1) * count]
        pieces = []
        for s in range(RING):
            at = slice(s * slots, (s + 1) * slots)
            pieces += [even[:, at], odd[:, at]]
        out[...] = jnp.concatenate(pieces, axis=1).astype(BF16).reshape(out.shape)


def pack_amplitudes_kernel(
    occ_ref,
    si_ref,
    sk_ref,
    lv_ref,
    rank_ref,
    amp_ref,
    pa_ref,
    hot_main,
    hot_rest,
    own_label,
    kept,
):
    n = pl.program_id(0)
    n_k, n_i, rows, wide = amp_ref.shape
    half = hot_main.shape[1]
    groups = hot_rest.shape[0]
    lv = lv_ref[...].astype(F32).astype(BF16)

    @pl.when(n == 0)
    def _():
        rank = rank_ref[...]
        hot_main[...] = one_hot(half, 0, rank).T
        for group in range(groups):
            hot_rest[group] = rest_hot(groups, group, half, rank).T
        own_label[...] = picked_column(lv_ref[...], lax.axis_index("blk") * rows, rows)

    for i in range(n_i):
        for k in range(n_k):
            label = jnp.bitwise_xor(occ_ref[sk_ref[n * n_k + k]], occ_ref[si_ref[i]])
            masked_rows(kept, i * n_k + k, label, own_label[...], lv, amp_ref[k, i])
    main = jnp.dot(kept[...], hot_main[...], preferred_element_type=F32).astype(BF16)
    count = n_i * n_k * rows // groups
    rest = jnp.zeros((count, half), F32)
    for group in range(groups):
        block = kept[group * count : (group + 1) * count]
        rest += jnp.dot(block, hot_rest[group], preferred_element_type=F32)
    main = main.reshape(n_i, n_k, rows, half)
    rest = rest.astype(BF16).reshape(n_i // groups, n_k, rows, half)
    for d in range(RING):
        for k in range(n_k):
            pa_ref[d, k, :n_i] = main[:, k]
            pa_ref[d, k, n_i:] = rest[:, k]


def unpack_kernel(
    occ_ref, si_ref, sk_ref, lv_ref, rank_ref, pa_ref, out_ref, hot, order, labels
):
    x, y, core, _ = coords()
    k = pl.program_id(0)
    n_rest, rows, half = pa_ref.shape[2:]
    groups = hot.shape[0]
    n_i = n_rest * groups // (groups + 1)
    wide = lv_ref.shape[1]

    @pl.when(k == 0)
    def _():
        p = iota((1, wide), 1)
        source = (
            ((x - (p // (4 * rows)) % RING + RING) % RING) * (rows * 8)
            + ((y - (p // rows) % RING + RING) % RING) * (rows * 2)
            + jnp.bitwise_xor(core, p // (wide // 2)) * rows
            + p % rows
        )
        pick = (iota((wide, wide), 0) == source).astype(F32).astype(BF16)
        which = iota((16, wide), 0)
        both = jnp.where(
            which == 0,
            jnp.broadcast_to(lv_ref[...], (16, wide)),
            jnp.broadcast_to(jnp.minimum(rank_ref[...], 255), (16, wide)),
        )
        moved = jnp.dot(both.astype(F32).astype(BF16), pick, preferred_element_type=F32).astype(I32)
        order[...] = moved[0:1].astype(F32).astype(BF16)
        rank = moved[1:2]
        main = one_hot(half, 0, rank)
        for side in range(groups):
            hot[side, :half] = main
            hot[side, half:] = rest_hot(groups, side, half, rank)
        for d in range(RING):
            first = x * (rows * 8) + ((y - d + RING) % RING) * (rows * 2) + core * rows
            labels[d] = picked_column(lv_ref[...], first, rows)

    lk = occ_ref[sk_ref[k]]
    group = n_i // groups
    blocks = [pa_ref.at[(y - d + RING) % RING] for d in range(RING)]
    for side in range(groups):
        pairs = []
        for block in blocks:
            main = block[0, side * group : (side + 1) * group].reshape(group * rows, half)
            rest = block[0, n_i:].reshape(group * rows, half)
            pairs.append(jnp.concatenate([main, rest], axis=1))
        spread = jnp.dot(
            jnp.concatenate(pairs, axis=0), hot[side], preferred_element_type=F32
        )
        for d in range(RING):
            for g in range(group):
                i = side * group + g
                label = jnp.bitwise_xor(lk, occ_ref[si_ref[i]])
                wanted = jnp.bitwise_xor(labels[d], label).astype(F32).astype(BF16)
                at = (d * n_i + i) * rows
                source = (d * group + g) * rows
                out_ref[0, at : at + rows, :] = jnp.where(
                    wanted == order[...],
                    spread[source : source + rows].astype(BF16),
                    jnp.zeros((), BF16),
                )


def folded(value, n_i, rows):
    used = value.shape[1]
    blocks = [value[n * rows : (n + 1) * rows] for n in range(value.shape[0] // rows)]
    if used == LANES:
        return blocks
    hosts = used // (LANES - used)
    held = n_i * hosts // (hosts + 1)
    out = []
    for d in range(len(blocks) // n_i):
        for i in range(held):
            guest = blocks[d * n_i + held + i // hosts]
            at = (i % hosts) * (LANES - used)
            out.append(
                jnp.concatenate([blocks[d * n_i + i], guest[:, at : at + LANES - used]], axis=1)
            )
    return out


def cycle_kernel(
    n_i, slots, first, a_ref, b0, b1, b2, b3, b4, b5, b6, b7, o0, o1, b_all, total
):
    k = pl.program_id(0)
    rows = b0.shape[2]
    depth = b0.shape[0] * rows
    start = first * CORES * slots // LANES * LANES
    for n, b in enumerate((b0, b1, b2, b3, b4, b5, b6, b7)):
        b_all[n * depth : (n + 1) * depth, :] = b[:, 0, :, start : start + 256].reshape(depth, 256)
    term = jnp.dot(a_ref[0], b_all[...], preferred_element_type=F32)

    @pl.when(k == 0)
    def _():
        total[...] = term

    @pl.when(jnp.logical_and(k > 0, k < pl.num_programs(0) - 1))
    def _():
        total[...] += term

    @pl.when(k == pl.num_programs(0) - 1)
    def _():
        full = total[...] + term
        for n, out in enumerate((o0, o1)):
            at = (first + n) * CORES * slots - start
            for m, block in enumerate(folded(full[:, at : at + CORES * slots], n_i, rows)):
                out[m // out.shape[1], m % out.shape[1]] = block


def sum_kernel(o0, o1, o2, o3, s0, s1, s2, s3):
    for d, out in enumerate((s0, s1, s2, s3)):
        out[...] = ((o0[d] + o1[d]) + o2[d]) + o3[d]


def update_kernel(
    slots,
    occ_ref,
    si_ref,
    sj_ref,
    oe_ref,
    lv_ref,
    ve_ref,
    part_ref,
    t0,
    t1,
    t2,
    t3,
    int_ref,
    out_ref,
    hot,
    own_label,
    own_energy,
    three,
):
    _, y, _, z = coords()
    n = pl.program_id(0)
    held, rows, lanes = t0.shape
    n_i, _, _, kept = int_ref.shape
    cols = pl.ds(pl.multiple_of(z * kept, kept), kept)

    @pl.when(n == 0)
    def _():
        slot = iota((lanes, kept), 0)
        part = part_ref[:, cols]
        for jj in range(CORES):
            one = (slot == part + jj * slots).astype(F32).astype(BF16)
            for n in range(3):
                hot[n * lanes : (n + 1) * lanes, jj * kept : (jj + 1) * kept] = one
        first = lax.axis_index("blk") * rows
        own_label[...] = picked_column(lv_ref[...], first, rows)
        own_energy[...] = picked_column(ve_ref[...], first, rows)

    spare = lanes - CORES * slots

    @pl.when(n == 0)
    def _():
        for d, t in enumerate((t0, t1, t2, t3)):
            for i in range(three.shape[0]):
                if i < held:
                    x = t[i]
                else:
                    hosts = CORES * slots // spare
                    first_host = (i - held) * hosts
                    x = jnp.concatenate(
                        [t[first_host + h][:, lanes - spare :] for h in range(hosts)]
                        + [jnp.zeros((rows, spare), F32)],
                        axis=1,
                    )
                top = x.astype(BF16)
                left = x - top.astype(F32)
                mid = left.astype(BF16)
                low = (left - mid.astype(F32)).astype(BF16)
                three[i, d * rows : (d + 1) * rows] = jnp.concatenate([top, mid, low], axis=1)

    label_b = lv_ref[:, cols]
    energy_b = ve_ref[:, cols]
    for e in range(n_i):
        i = n * n_i + e
        cycle = jnp.dot(three[i], hot[...], preferred_element_type=F32)
        label_i = occ_ref[si_ref[i]]
        energy_i = oe_ref[si_ref[i]]
        for d in range(RING):
            for jj in range(CORES):
                j = ((y + d) % RING) * CORES + jj
                label = jnp.bitwise_xor(label_i, occ_ref[sj_ref[j]])
                denom = ((energy_i + oe_ref[sj_ref[j]]) - own_energy[...]) - energy_b
                term = cycle[d * rows : (d + 1) * rows, jj * kept : (jj + 1) * kept]
                value = (int_ref[e, j].astype(F32) + term) / denom
                keep = jnp.bitwise_xor(own_label[...], label) == label_b
                out_ref[e, j] = jnp.where(keep, value, 0.0)


SMEM = pl.BlockSpec(memory_space=pltpu.SMEM)


def whole(shape):
    return pl.BlockSpec(shape, lambda n: (0,) * len(shape))


def cost(flops, moved):
    return pl.CostEstimate(flops=flops, bytes_accessed=moved, transcendentals=0)


def halves(shape, dim):
    block = tuple(size // 2 if at == dim else size for at, size in enumerate(shape))
    return pl.BlockSpec(block, lambda n: tuple(n if at == dim else 0 for at in range(len(shape))))


def pack_dressed(slots, dressed, occ_irrep, virt_irrep, slab_j, slab_k):
    n_k, n_j, rows, wide = dressed.shape
    out = (n_k, rows, RING * CORES * slots)
    row_spec = whole((1, wide))
    row = jax.ShapeDtypeStruct((1, wide), I32)
    *pb, rank, part, fits = pl.pallas_call(
        functools.partial(pack_dressed_kernel, slots),
        grid=(2,),
        out_shape=[jax.ShapeDtypeStruct(out, BF16)] * RING
        + [row, row, jax.ShapeDtypeStruct((1,), I32)],
        in_specs=[SMEM] * 3 + [row_spec, halves(dressed.shape, 0)],
        out_specs=[halves(out, 0)] * RING + [row_spec, row_spec, SMEM],
        scratch_shapes=[
            pltpu.VMEM((wide, RING * slots), BF16),
            pltpu.VMEM((rows, 1), I32),
            pltpu.VMEM((n_k * n_j * rows // 2, wide), BF16),
        ],
        compiler_params=pltpu.CompilerParams(vmem_limit_bytes=32 * 1024 * 1024),
        cost_estimate=cost(2 * n_k * n_j * rows * wide * 256, 10 << 20),
        name="pack_dressed",
    )(occ_irrep, slab_j, slab_k, virt_irrep.reshape(1, wide), dressed)
    return pb, rank, part, fits


def pack_amplitudes(slots, amplitudes, rank, occ_irrep, virt_irrep, slab_i, slab_k):
    n_k, n_i, rows, wide = amplitudes.shape
    half = LANES
    groups = half // (slots - half)
    out = (RING, n_k, n_i + n_i // groups, rows, half)
    row_spec = whole((1, wide))
    return pl.pallas_call(
        pack_amplitudes_kernel,
        grid=(2,),
        out_shape=jax.ShapeDtypeStruct(out, BF16),
        in_specs=[SMEM] * 3 + [row_spec, row_spec, halves(amplitudes.shape, 0)],
        out_specs=halves(out, 1),
        scratch_shapes=[
            pltpu.VMEM((wide, half), BF16),
            pltpu.VMEM((groups, wide, half), BF16),
            pltpu.VMEM((rows, 1), I32),
            pltpu.VMEM((n_k * n_i * rows // 2, wide), BF16),
        ],
        compiler_params=pltpu.CompilerParams(vmem_limit_bytes=32 * 1024 * 1024),
        cost_estimate=cost(2 * n_k * n_i * rows * wide * 256, 10 << 20),
        name="pack_amplitudes",
    )(occ_irrep, slab_i, slab_k, virt_irrep.reshape(1, wide), rank, amplitudes)


def ring_y(d):
    return [
        (8 * x + 2 * y + c, 8 * x + 2 * ((y + d) % RING) + c)
        for x in range(RING)
        for y in range(RING)
        for c in range(CORES)
    ]


def groups_y():
    return [
        [8 * x + 2 * y + c for y in range(RING)] for x in range(RING) for c in range(CORES)
    ]


def ring_x(d):
    return [
        (8 * x + m, 8 * ((x + d) % RING) + m) for x in range(RING) for m in range(RING * CORES)
    ]


def ring_z(d):
    return [(z, (z + d) % RING) for z in range(RING)]


def other_core():
    return [(b, b ^ 1) for b in range(RING * RING * CORES)]


def over_y(pb):
    return [pb[0]] + [lax.ppermute(pb[d], "blk", ring_y(d)) for d in (1, 2, 3)]


def packed_form(
    slots,
    pb_y,
    pa,
    rank,
    part,
    amplitudes,
    integrals,
    occ_irrep,
    virt_irrep,
    occ_energy,
    virt_energy,
    slab_i,
    slab_j,
    slab_k,
):
    n_k, n_i, rows, wide = amplitudes.shape
    n_j = integrals.shape[1]
    kept = integrals.shape[3]
    half = LANES
    n_rest = pa.shape[2]
    groups = n_i // (n_rest - n_i)
    n_cols = RING * CORES * slots
    held = n_i * CORES * slots // LANES
    lv = virt_irrep.reshape(1, wide)
    ve = virt_energy.reshape(1, wide)
    row_spec = whole((1, wide))
    params = pltpu.CompilerParams(vmem_limit_bytes=32 * 1024 * 1024)

    pa_y = lax.all_to_all(pa, "blk", 0, 0, axis_index_groups=groups_y())

    m_rows = RING * n_i * rows
    spread = pl.pallas_call(
        unpack_kernel,
        grid=(n_k,),
        out_shape=jax.ShapeDtypeStruct((n_k, m_rows, wide), BF16),
        in_specs=[SMEM] * 3
        + [row_spec] * 2
        + [pl.BlockSpec((RING, 1, n_rest, rows, half), lambda k: (0, k, 0, 0, 0))],
        out_specs=pl.BlockSpec((1, m_rows, wide), lambda k: (k, 0, 0)),
        scratch_shapes=[
            pltpu.VMEM((groups, 2 * half, wide), BF16),
            pltpu.VMEM((1, wide), BF16),
            pltpu.VMEM((RING, rows, 1), I32),
        ],
        compiler_params=params,
        cost_estimate=cost(2 * n_k * m_rows * wide * 256, 20 << 20),
        name="unpack",
    )(occ_irrep, slab_i, slab_k, lv, rank, pa_y)

    mine = jnp.stack(pb_y)
    across = [mine] + [lax.ppermute(mine, "blk", ring_x(d)) for d in (1, 2, 3)]
    *across[2:], spread = lax.optimization_barrier((*across[2:], spread))
    twin = [lax.ppermute(b, "blk", other_core()) for b in across]
    parts = {}
    for first in (0, 2):
        parts[STEPS[first]], parts[STEPS[first + 1]] = pl.pallas_call(
            functools.partial(cycle_kernel, n_i, slots, first),
            grid=(n_k,),
            out_shape=[jax.ShapeDtypeStruct((RING, held, rows, LANES), F32)] * 2,
            in_specs=[pl.BlockSpec((1, m_rows, wide), lambda k: (k, 0, 0))]
            + [pl.BlockSpec((RING, 1, rows, n_cols), lambda k: (0, k, 0, 0))] * 8,
            out_specs=[whole((RING, held, rows, LANES))] * 2,
            scratch_shapes=[pltpu.VMEM((wide, 256), BF16), pltpu.VMEM((m_rows, 256), F32)],
            compiler_params=params,
            cost_estimate=cost(2 * n_k * m_rows * wide * 256, 14 << 20),
            name="cycle",
        )(spread, *across, *twin)

    sums = [parts[0]] + [lax.ppermute(parts[d], "red", ring_z(d)) for d in (1, 2, 3)]
    terms = pl.pallas_call(
        sum_kernel,
        grid=(2,),
        out_shape=[jax.ShapeDtypeStruct((held, rows, LANES), F32)] * RING,
        in_specs=[pl.BlockSpec((RING, held // 2, rows, LANES), lambda n: (0, n, 0, 0))] * RING,
        out_specs=[pl.BlockSpec((held // 2, rows, LANES), lambda n: (n, 0, 0))] * RING,
        compiler_params=params,
        cost_estimate=cost(m_rows * 512, 3 << 20),
        name="sums",
    )(*sums)
    back = [terms[0]] + [lax.ppermute(terms[d], "blk", ring_y(RING - d)) for d in (1, 2, 3)]

    return pl.pallas_call(
        functools.partial(update_kernel, slots),
        grid=(n_i // 2,),
        out_shape=jax.ShapeDtypeStruct(integrals.shape, F32),
        in_specs=[SMEM] * 4
        + [row_spec] * 3
        + [whole((held, rows, LANES))] * RING
        + [pl.BlockSpec((2, n_j, rows, kept), lambda n: (n, 0, 0, 0))],
        out_specs=pl.BlockSpec((2, n_j, rows, kept), lambda n: (n, 0, 0, 0)),
        scratch_shapes=[
            pltpu.VMEM((3 * LANES, CORES * kept), BF16),
            pltpu.VMEM((rows, 1), I32),
            pltpu.VMEM((rows, 1), F32),
            pltpu.VMEM((n_i, RING * rows, 3 * LANES), BF16),
        ],
        compiler_params=params,
        cost_estimate=cost(2 * 3 * m_rows * 128 * 512, 4 << 20),
        name="update",
    )(occ_irrep, slab_i, slab_j, occ_energy, lv, ve, part, *back, integrals)


def on_device(
    amplitudes,
    dressed,
    integrals,
    occ_irrep,
    virt_irrep,
    occ_energy,
    virt_energy,
    slab_i,
    slab_j,
    slab_k,
):
    pb_y, rank, part, fits = pack_dressed(
        PARTS[1], dressed, occ_irrep, virt_irrep, slab_j, slab_k
    )
    pb_y = over_y(pb_y)
    pa = pack_amplitudes(WIDES[1], amplitudes, rank, occ_irrep, virt_irrep, slab_i, slab_k)
    rest = (integrals, occ_irrep, virt_irrep, occ_energy, virt_energy, slab_i, slab_j, slab_k)

    def dense(pb_y, pa, rank, part, fits, a, d, *rest):
        return dense_form(a, d, *rest)

    def loose(pb_y, pa, rank, part, fits, a, d, *rest):
        pb, rank, part, _ = pack_dressed(PARTS[0], d, rest[1], rest[2], rest[6], rest[7])
        pa = pack_amplitudes(WIDES[0], a, rank, rest[1], rest[2], rest[5], rest[7])
        return packed_form(PARTS[0], over_y(pb), pa, rank, part, a, *rest)

    def tight(pb_y, pa, rank, part, fits, a, d, *rest):
        return packed_form(PARTS[1], pb_y, pa, rank, part, a, *rest)

    def other(pb_y, pa, rank, part, fits, *arrays):
        return lax.cond(fits[0] == 1, loose, dense, pb_y, pa, rank, part, fits, *arrays)

    return lax.cond(
        fits[0] == 2, tight, other, pb_y, pa, rank, part, fits, amplitudes, dressed, *rest
    )


def solution(mesh):
    in_specs = (
        P("red", None, "blk", None),
        P("red", None, "blk", None),
        P(None, None, "blk", "red"),
        P(),
        P(),
        P(),
        P(),
        P(),
        P(),
        P("red"),
    )
    out_specs = P(None, None, "blk", "red")
    return jax.shard_map(
        on_device, mesh=mesh, in_specs=in_specs, out_specs=out_specs, check_vma=False
    )
```

```python
import functools

import jax
import jax.numpy as jnp
import numpy as np
from jax import lax
from jax.experimental import pallas as pl
from jax.experimental.pallas import tpu as pltpu
from jax.sharding import PartitionSpec as P

F32 = jnp.float32
BF16 = jnp.bfloat16
I32 = jnp.int32

RING = 4
CORES = 2
WIDES = (192, 160)
PARTS = (64, 48)
STEPS = (1, 3, 2, 0)
LANES = 128


def table_lookup(table, picks):
    hits = picks[:, None] == jnp.arange(table.shape[0], dtype=jnp.int32)[None, :]
    return jnp.sum(jnp.where(hits, table[None, :], jnp.zeros((), table.dtype)), axis=1)


def dense_form(
    amplitudes,
    dressed,
    integrals,
    occ_irrep,
    virt_irrep,
    occ_energy,
    virt_energy,
    slab_i,
    slab_j,
    slab_k,
):
    blk_size = lax.axis_size("blk")
    red_size = lax.axis_size("red")
    k_local, slab_rows, virt_rows, virt_all = amplitudes.shape
    occ_cols = dressed.shape[1]
    cols_kept = virt_all // red_size
    pair_count = slab_rows * occ_cols // blk_size
    own_rows = max(1, pair_count // occ_cols)
    own_cols = min(pair_count, occ_cols)
    owners = np.arange(blk_size)
    first_pair = owners * pair_count
    table_rows = ((first_pair // occ_cols)[:, None] + np.arange(own_rows)[None, :]).reshape(-1)
    table_cols = ((first_pair % occ_cols)[:, None] + np.arange(own_cols)[None, :]).reshape(-1)
    blk_place = lax.axis_index("blk")
    red_place = lax.axis_index("red")
    label_i = table_lookup(occ_irrep, slab_i)
    label_j = table_lookup(occ_irrep, slab_j)
    label_k = table_lookup(occ_irrep, slab_k)
    rows_label = lax.dynamic_slice_in_dim(virt_irrep, blk_place * virt_rows, virt_rows)
    pair_virt = jnp.bitwise_xor(rows_label[:, None], virt_irrep[None, :])
    amp_sym = jnp.bitwise_xor(
        jnp.bitwise_xor(label_k[:, None], label_i[None, :])[:, :, None, None], pair_virt[None, None]
    )
    kept_amp = jnp.where(amp_sym == 0, amplitudes, jnp.zeros((), amplitudes.dtype))
    dre_sym = jnp.bitwise_xor(
        jnp.bitwise_xor(label_k[:, None], label_j[None, :])[:, :, None, None], pair_virt[None, None]
    )
    kept_dre = jnp.where(dre_sym == 0, dressed, jnp.zeros((), dressed.dtype))
    send_amp = jnp.take(kept_amp, table_rows, axis=1).reshape(
        k_local, blk_size, own_rows, virt_rows, virt_all
    )
    send_dre = jnp.take(kept_dre, table_cols, axis=1).reshape(
        k_local, blk_size, own_cols, virt_rows, virt_all
    )
    amp_owner = lax.all_to_all(send_amp, "blk", split_axis=1, concat_axis=3, tiled=True)[:, 0]
    dre_owner = lax.all_to_all(send_dre, "blk", split_axis=1, concat_axis=3, tiled=True)[:, 0]
    partial_cycle = jnp.einsum(
        "kiac,kjcb->ijab", amp_owner, dre_owner, preferred_element_type=jnp.float32
    )
    by_cols = partial_cycle.reshape(pair_count, virt_all, red_size, cols_kept)
    cycle_pairs = lax.all_to_all(by_cols, "red", split_axis=2, concat_axis=2, tiled=True).sum(axis=2)
    cycle_kept = lax.all_to_all(
        cycle_pairs, "blk", split_axis=1, concat_axis=0, tiled=True
    ).reshape(slab_rows, occ_cols, virt_rows, cols_kept)
    energy_i = table_lookup(occ_energy, slab_i)
    energy_j = table_lookup(occ_energy, slab_j)
    energy_a = lax.dynamic_slice_in_dim(virt_energy, blk_place * virt_rows, virt_rows)
    energy_b = lax.dynamic_slice_in_dim(virt_energy, red_place * cols_kept, cols_kept)
    label_b = lax.dynamic_slice_in_dim(virt_irrep, red_place * cols_kept, cols_kept)
    denom = (
        energy_i[:, None, None, None]
        + energy_j[None, :, None, None]
        - energy_a[None, None, :, None]
        - energy_b[None, None, None, :]
    )
    out_virt = jnp.bitwise_xor(rows_label[:, None], label_b[None, :])
    out_sym = jnp.bitwise_xor(
        jnp.bitwise_xor(label_i[:, None], label_j[None, :])[:, :, None, None], out_virt[None, None]
    )
    value = (integrals.astype(jnp.float32) + cycle_kept) / denom
    return jnp.where(out_sym == 0, value, jnp.zeros((), jnp.float32))


def coords():
    blk = lax.axis_index("blk")
    return blk // (RING * CORES), (blk // CORES) % RING, blk % CORES, lax.axis_index("red")


def iota(shape, dim):
    return lax.broadcasted_iota(I32, shape, dim)


def picked_column(row, first, count):
    wide = row.shape[1]
    hit = iota((count, wide), 1) == iota((count, wide), 0) + first
    kept = jnp.where(hit, jnp.broadcast_to(row.astype(F32), (count, wide)), 0.0)
    return jnp.sum(kept, axis=1, keepdims=True).astype(row.dtype)


def one_hot(count, first, row):
    slot = (iota((count, 1), 0) + first).astype(F32).astype(BF16)
    there = jnp.clip(row, -1, 256).astype(F32).astype(BF16)
    return jnp.where(slot == there, jnp.ones((), BF16), jnp.zeros((), BF16))


def rest_hot(groups, group, half, rank):
    share = half // groups
    slot = iota((half, 1), 0) - group * share
    inside = jnp.logical_and(slot >= 0, slot < share)
    slot = jnp.where(inside, slot + half, 512).astype(F32).astype(BF16)
    there = jnp.clip(rank, -1, 256).astype(F32).astype(BF16)
    return jnp.where(slot == there, jnp.ones((), BF16), jnp.zeros((), BF16))


def label_ranks(lv_ref, rank_ref, part_ref, fits_ref):
    wide = lv_ref.shape[1]
    quarter = wide // RING
    tri = (iota((quarter, quarter), 0) < iota((quarter, quarter), 1)).astype(F32).astype(BF16)
    base = jnp.zeros((16, 1), F32)
    most_part = jnp.zeros((1, 1), F32)
    for part in range(RING):
        lanes = slice(part * quarter, (part + 1) * quarter)
        member = (iota((16, quarter), 0) == lv_ref[:, lanes]).astype(F32)
        before = jnp.dot(member.astype(BF16), tri, preferred_element_type=F32)
        part_ref[:, lanes] = jnp.sum(member * before, axis=0, keepdims=True).astype(I32)
        rank_ref[:, lanes] = jnp.sum(member * (before + base), axis=0, keepdims=True).astype(I32)
        count = jnp.sum(member, axis=1, keepdims=True)
        most_part = jnp.maximum(most_part, jnp.max(count))
        base = base + count
    most = jnp.max(most_part)
    whole_most = jnp.max(base)
    fits = jnp.logical_and(whole_most <= WIDES[0], most <= PARTS[0])
    tight = jnp.logical_and(whole_most <= WIDES[1], most <= PARTS[1])
    fits_ref[0] = fits.astype(I32) + tight.astype(I32)


def masked_rows(kept, at, label, own_label, lv, block):
    rows = block.shape[0]
    wanted = jnp.bitwise_xor(own_label, label).astype(F32).astype(BF16)
    kept[at * rows : (at + 1) * rows, :] = jnp.where(wanted == lv, block, jnp.zeros((), BF16))


def pack_dressed_kernel(
    slots,
    occ_ref,
    sj_ref,
    sk_ref,
    lv_ref,
    dre_ref,
    p0,
    p1,
    p2,
    p3,
    rank_ref,
    part_ref,
    fits_ref,
    hot_part,
    own_label,
    kept,
):
    _, y, _, z = coords()
    n = pl.program_id(0)
    n_k, _, rows, wide = dre_ref.shape
    lv = lv_ref[...].astype(F32).astype(BF16)

    @pl.when(n == 0)
    def _():
        label_ranks(lv_ref, rank_ref, part_ref, fits_ref)
        step = (iota((1, wide), 1) // (wide // RING) - z + RING) % RING
        first = jnp.zeros((1, wide), I32)
        for n_step, s in enumerate(STEPS):
            first = jnp.where(step == s, n_step * slots, first)
        place = first + jnp.minimum(part_ref[...], slots - 1)
        hot_part[...] = one_hot(RING * slots, 0, place).T
        own_label[...] = picked_column(lv_ref[...], lax.axis_index("blk") * rows, rows)

    for k in range(n_k):
        lk = occ_ref[sk_ref[n * n_k + k]]
        for d in range(RING):
            for jj in range(CORES):
                j = ((y + d) % RING) * CORES + jj
                label = jnp.bitwise_xor(lk, occ_ref[sj_ref[j]])
                at = (jj * RING + d) * n_k + k
                masked_rows(kept, at, label, own_label[...], lv, dre_ref[k, j])
    count = n_k * rows
    packed = jnp.dot(kept[...], hot_part[...], preferred_element_type=F32)
    for d, out in enumerate((p0, p1, p2, p3)):
        even = packed[d * count : (d + 1) * count]
        odd = packed[(RING + d) * count : (RING + d + 1) * count]
        pieces = []
        for s in range(RING):
            at = slice(s * slots, (s + 1) * slots)
            pieces += [even[:, at], odd[:, at]]
        out[...] = jnp.concatenate(pieces, axis=1).astype(BF16).reshape(out.shape)


def pack_amplitudes_kernel(
    occ_ref,
    si_ref,
    sk_ref,
    lv_ref,
    rank_ref,
    amp_ref,
    pa_ref,
    hot_main,
    hot_rest,
    own_label,
    kept,
):
    n = pl.program_id(0)
    n_k, n_i, rows, wide = amp_ref.shape
    half = hot_main.shape[1]
    groups = hot_rest.shape[0]
    lv = lv_ref[...].astype(F32).astype(BF16)

    @pl.when(n == 0)
    def _():
        rank = rank_ref[...]
        hot_main[...] = one_hot(half, 0, rank).T
        for group in range(groups):
            hot_rest[group] = rest_hot(groups, group, half, rank).T
        own_label[...] = picked_column(lv_ref[...], lax.axis_index("blk") * rows, rows)

    for i in range(n_i):
        for k in range(n_k):
            label = jnp.bitwise_xor(occ_ref[sk_ref[n * n_k + k]], occ_ref[si_ref[i]])
            masked_rows(kept, i * n_k + k, label, own_label[...], lv, amp_ref[k, i])
    main = jnp.dot(kept[...], hot_main[...], preferred_element_type=F32).astype(BF16)
    count = n_i * n_k * rows // groups
    rest = jnp.zeros((count, half), F32)
    for group in range(groups):
        block = kept[group * count : (group + 1) * count]
        rest += jnp.dot(block, hot_rest[group], preferred_element_type=F32)
    main = main.reshape(n_i, n_k, rows, half)
    rest = rest.astype(BF16).reshape(n_i // groups, n_k, rows, half)
    for d in range(RING):
        for k in range(n_k):
            pa_ref[d, k, :n_i] = main[:, k]
            pa_ref[d, k, n_i:] = rest[:, k]


def unpack_kernel(
    occ_ref, si_ref, sk_ref, lv_ref, rank_ref, pa_ref, out_ref, hot, order, labels
):
    x, y, core, _ = coords()
    k = pl.program_id(0)
    n_rest, rows, half = pa_ref.shape[2:]
    groups = hot.shape[0]
    n_i = n_rest * groups // (groups + 1)
    wide = lv_ref.shape[1]

    @pl.when(k == 0)
    def _():
        p = iota((1, wide), 1)
        source = (
            ((x - (p // (4 * rows)) % RING + RING) % RING) * (rows * 8)
            + ((y - (p // rows) % RING + RING) % RING) * (rows * 2)
            + jnp.bitwise_xor(core, p // (wide // 2)) * rows
            + p % rows
        )
        pick = (iota((wide, wide), 0) == source).astype(F32).astype(BF16)
        which = iota((16, wide), 0)
        both = jnp.where(
            which == 0,
            jnp.broadcast_to(lv_ref[...], (16, wide)),
            jnp.broadcast_to(jnp.minimum(rank_ref[...], 255), (16, wide)),
        )
        moved = jnp.dot(both.astype(F32).astype(BF16), pick, preferred_element_type=F32).astype(I32)
        order[...] = moved[0:1].astype(F32).astype(BF16)
        rank = moved[1:2]
        main = one_hot(half, 0, rank)
        for side in range(groups):
            hot[side, :half] = main
            hot[side, half:] = rest_hot(groups, side, half, rank)
        for d in range(RING):
            first = x * (rows * 8) + ((y - d + RING) % RING) * (rows * 2) + core * rows
            labels[d] = picked_column(lv_ref[...], first, rows)

    for e in range(out_ref.shape[0]):
        lk = occ_ref[sk_ref[k * out_ref.shape[0] + e]]
        group = n_i // groups
        blocks = [pa_ref.at[(y - d + RING) % RING] for d in range(RING)]
        for side in range(groups):
            pairs = []
            for block in blocks:
                main = block[e, side * group : (side + 1) * group].reshape(group * rows, half)
                rest = block[e, n_i:].reshape(group * rows, half)
                pairs.append(jnp.concatenate([main, rest], axis=1))
            spread = jnp.dot(
                jnp.concatenate(pairs, axis=0), hot[side], preferred_element_type=F32
            )
            for d in range(RING):
                for g in range(group):
                    i = side * group + g
                    label = jnp.bitwise_xor(lk, occ_ref[si_ref[i]])
                    wanted = jnp.bitwise_xor(labels[d], label).astype(F32).astype(BF16)
                    at = (d * n_i + i) * rows
                    source = (d * group + g) * rows
                    out_ref[e, at : at + rows, :] = jnp.where(
                        wanted == order[...],
                        spread[source : source + rows].astype(BF16),
                        jnp.zeros((), BF16),
                    )


def folded(value, n_i, rows):
    used = value.shape[1]
    blocks = [value[n * rows : (n + 1) * rows] for n in range(value.shape[0] // rows)]
    if used == LANES:
        return blocks
    hosts = used // (LANES - used)
    held = n_i * hosts // (hosts + 1)
    out = []
    for d in range(len(blocks) // n_i):
        for i in range(held):
            guest = blocks[d * n_i + held + i // hosts]
            at = (i % hosts) * (LANES - used)
            out.append(
                jnp.concatenate([blocks[d * n_i + i], guest[:, at : at + LANES - used]], axis=1)
            )
    return out


def cycle_kernel(
    n_i, slots, first, a_ref, b0, b1, b2, b3, b4, b5, b6, b7, o0, o1, b_all, total
):
    k = pl.program_id(0)
    rows = b0.shape[2]
    depth = b0.shape[0] * rows
    start = first * CORES * slots // LANES * LANES
    term = None
    for e in range(a_ref.shape[0]):
        for n, b in enumerate((b0, b1, b2, b3, b4, b5, b6, b7)):
            block = b[:, e, :, start : start + 256].reshape(depth, 256)
            b_all[e, n * depth : (n + 1) * depth, :] = block
        part = jnp.dot(a_ref[e], b_all[e], preferred_element_type=F32)
        term = part if term is None else term + part

    @pl.when(k == 0)
    def _():
        total[...] = term

    @pl.when(jnp.logical_and(k > 0, k < pl.num_programs(0) - 1))
    def _():
        total[...] += term

    @pl.when(k == pl.num_programs(0) - 1)
    def _():
        full = total[...] + term
        for n, out in enumerate((o0, o1)):
            at = (first + n) * CORES * slots - start
            for m, block in enumerate(folded(full[:, at : at + CORES * slots], n_i, rows)):
                out[m // out.shape[1], m % out.shape[1]] = block


def sum_kernel(o0, o1, o2, o3, s0, s1, s2, s3):
    for d, out in enumerate((s0, s1, s2, s3)):
        out[...] = ((o0[d] + o1[d]) + o2[d]) + o3[d]


def update_kernel(
    slots,
    occ_ref,
    si_ref,
    sj_ref,
    oe_ref,
    lv_ref,
    ve_ref,
    part_ref,
    t0,
    t1,
    t2,
    t3,
    int_ref,
    out_ref,
    hot,
    own_label,
    own_energy,
    three,
):
    _, y, _, z = coords()
    n = pl.program_id(0)
    held, rows, lanes = t0.shape
    n_i, _, _, kept = int_ref.shape
    cols = pl.ds(pl.multiple_of(z * kept, kept), kept)

    @pl.when(n == 0)
    def _():
        slot = iota((lanes, kept), 0)
        part = part_ref[:, cols]
        for jj in range(CORES):
            one = (slot == part + jj * slots).astype(F32).astype(BF16)
            for n in range(3):
                hot[n * lanes : (n + 1) * lanes, jj * kept : (jj + 1) * kept] = one
        first = lax.axis_index("blk") * rows
        own_label[...] = picked_column(lv_ref[...], first, rows)
        own_energy[...] = picked_column(ve_ref[...], first, rows)

    spare = lanes - CORES * slots

    @pl.when(n == 0)
    def _():
        for d, t in enumerate((t0, t1, t2, t3)):
            for i in range(three.shape[0]):
                if i < held:
                    x = t[i]
                else:
                    hosts = CORES * slots // spare
                    first_host = (i - held) * hosts
                    x = jnp.concatenate(
                        [t[first_host + h][:, lanes - spare :] for h in range(hosts)]
                        + [jnp.zeros((rows, spare), F32)],
                        axis=1,
                    )
                top = x.astype(BF16)
                left = x - top.astype(F32)
                mid = left.astype(BF16)
                low = (left - mid.astype(F32)).astype(BF16)
                three[i, d * rows : (d + 1) * rows] = jnp.concatenate([top, mid, low], axis=1)

    label_b = lv_ref[:, cols]
    energy_b = ve_ref[:, cols]
    for e in range(n_i):
        i = n * n_i + e
        cycle = jnp.dot(three[i], hot[...], preferred_element_type=F32)
        label_i = occ_ref[si_ref[i]]
        energy_i = oe_ref[si_ref[i]]
        for d in range(RING):
            for jj in range(CORES):
                j = ((y + d) % RING) * CORES + jj
                label = jnp.bitwise_xor(label_i, occ_ref[sj_ref[j]])
                denom = ((energy_i + oe_ref[sj_ref[j]]) - own_energy[...]) - energy_b
                term = cycle[d * rows : (d + 1) * rows, jj * kept : (jj + 1) * kept]
                value = (int_ref[e, j].astype(F32) + term) / denom
                keep = jnp.bitwise_xor(own_label[...], label) == label_b
                out_ref[e, j] = jnp.where(keep, value, 0.0)


SMEM = pl.BlockSpec(memory_space=pltpu.SMEM)


def whole(shape):
    return pl.BlockSpec(shape, lambda n: (0,) * len(shape))


def cost(flops, moved):
    return pl.CostEstimate(flops=flops, bytes_accessed=moved, transcendentals=0)


def halves(shape, dim):
    block = tuple(size // 2 if at == dim else size for at, size in enumerate(shape))
    return pl.BlockSpec(block, lambda n: tuple(n if at == dim else 0 for at in range(len(shape))))


def pack_dressed(slots, dressed, occ_irrep, virt_irrep, slab_j, slab_k):
    n_k, n_j, rows, wide = dressed.shape
    out = (n_k, rows, RING * CORES * slots)
    row_spec = whole((1, wide))
    row = jax.ShapeDtypeStruct((1, wide), I32)
    *pb, rank, part, fits = pl.pallas_call(
        functools.partial(pack_dressed_kernel, slots),
        grid=(2,),
        out_shape=[jax.ShapeDtypeStruct(out, BF16)] * RING
        + [row, row, jax.ShapeDtypeStruct((1,), I32)],
        in_specs=[SMEM] * 3 + [row_spec, halves(dressed.shape, 0)],
        out_specs=[halves(out, 0)] * RING + [row_spec, row_spec, SMEM],
        scratch_shapes=[
            pltpu.VMEM((wide, RING * slots), BF16),
            pltpu.VMEM((rows, 1), I32),
            pltpu.VMEM((n_k * n_j * rows // 2, wide), BF16),
        ],
        compiler_params=pltpu.CompilerParams(vmem_limit_bytes=32 * 1024 * 1024),
        cost_estimate=cost(2 * n_k * n_j * rows * wide * 256, 10 << 20),
        name="pack_dressed",
    )(occ_irrep, slab_j, slab_k, virt_irrep.reshape(1, wide), dressed)
    return pb, rank, part, fits


def pack_amplitudes(slots, amplitudes, rank, occ_irrep, virt_irrep, slab_i, slab_k):
    n_k, n_i, rows, wide = amplitudes.shape
    half = LANES
    groups = half // (slots - half)
    out = (RING, n_k, n_i + n_i // groups, rows, half)
    row_spec = whole((1, wide))
    return pl.pallas_call(
        pack_amplitudes_kernel,
        grid=(2,),
        out_shape=jax.ShapeDtypeStruct(out, BF16),
        in_specs=[SMEM] * 3 + [row_spec, row_spec, halves(amplitudes.shape, 0)],
        out_specs=halves(out, 1),
        scratch_shapes=[
            pltpu.VMEM((wide, half), BF16),
            pltpu.VMEM((groups, wide, half), BF16),
            pltpu.VMEM((rows, 1), I32),
            pltpu.VMEM((n_k * n_i * rows // 2, wide), BF16),
        ],
        compiler_params=pltpu.CompilerParams(vmem_limit_bytes=32 * 1024 * 1024),
        cost_estimate=cost(2 * n_k * n_i * rows * wide * 256, 10 << 20),
        name="pack_amplitudes",
    )(occ_irrep, slab_i, slab_k, virt_irrep.reshape(1, wide), rank, amplitudes)


def ring_y(d):
    return [
        (8 * x + 2 * y + c, 8 * x + 2 * ((y + d) % RING) + c)
        for x in range(RING)
        for y in range(RING)
        for c in range(CORES)
    ]


def groups_y():
    return [
        [8 * x + 2 * y + c for y in range(RING)] for x in range(RING) for c in range(CORES)
    ]


def ring_x(d):
    return [
        (8 * x + m, 8 * ((x + d) % RING) + m) for x in range(RING) for m in range(RING * CORES)
    ]


def ring_z(d):
    return [(z, (z + d) % RING) for z in range(RING)]


def other_core():
    return [(b, b ^ 1) for b in range(RING * RING * CORES)]


def over_y(pb):
    return [pb[0]] + [lax.ppermute(pb[d], "blk", ring_y(d)) for d in (1, 2, 3)]


def packed_form(
    slots,
    pb_y,
    pa,
    rank,
    part,
    amplitudes,
    integrals,
    occ_irrep,
    virt_irrep,
    occ_energy,
    virt_energy,
    slab_i,
    slab_j,
    slab_k,
):
    n_k, n_i, rows, wide = amplitudes.shape
    n_j = integrals.shape[1]
    kept = integrals.shape[3]
    half = LANES
    n_rest = pa.shape[2]
    groups = n_i // (n_rest - n_i)
    n_cols = RING * CORES * slots
    held = n_i * CORES * slots // LANES
    lv = virt_irrep.reshape(1, wide)
    ve = virt_energy.reshape(1, wide)
    row_spec = whole((1, wide))
    params = pltpu.CompilerParams(vmem_limit_bytes=32 * 1024 * 1024)

    pa_y = lax.all_to_all(pa, "blk", 0, 0, axis_index_groups=groups_y())

    m_rows = RING * n_i * rows
    spread = pl.pallas_call(
        unpack_kernel,
        grid=(n_k // 2,),
        out_shape=jax.ShapeDtypeStruct((n_k, m_rows, wide), BF16),
        in_specs=[SMEM] * 3
        + [row_spec] * 2
        + [pl.BlockSpec((RING, 2, n_rest, rows, half), lambda k: (0, k, 0, 0, 0))],
        out_specs=pl.BlockSpec((2, m_rows, wide), lambda k: (k, 0, 0)),
        scratch_shapes=[
            pltpu.VMEM((groups, 2 * half, wide), BF16),
            pltpu.VMEM((1, wide), BF16),
            pltpu.VMEM((RING, rows, 1), I32),
        ],
        compiler_params=params,
        cost_estimate=cost(2 * n_k * m_rows * wide * 256, 20 << 20),
        name="unpack",
    )(occ_irrep, slab_i, slab_k, lv, rank, pa_y)

    mine = jnp.stack(pb_y)
    across = [mine] + [lax.ppermute(mine, "blk", ring_x(d)) for d in (1, 2, 3)]
    *across[2:], spread = lax.optimization_barrier((*across[2:], spread))
    twin = [lax.ppermute(b, "blk", other_core()) for b in across]
    parts = {}
    for first in (0, 2):
        parts[STEPS[first]], parts[STEPS[first + 1]] = pl.pallas_call(
            functools.partial(cycle_kernel, n_i, slots, first),
            grid=(n_k // 2,),
            out_shape=[jax.ShapeDtypeStruct((RING, held, rows, LANES), F32)] * 2,
            in_specs=[pl.BlockSpec((2, m_rows, wide), lambda k: (k, 0, 0))]
            + [pl.BlockSpec((RING, 2, rows, n_cols), lambda k: (0, k, 0, 0))] * 8,
            out_specs=[whole((RING, held, rows, LANES))] * 2,
            scratch_shapes=[pltpu.VMEM((2, wide, 256), BF16), pltpu.VMEM((m_rows, 256), F32)],
            compiler_params=params,
            cost_estimate=cost(2 * n_k * m_rows * wide * 256, 14 << 20),
            name="cycle",
        )(spread, *across, *twin)

    sums = [parts[0]] + [lax.ppermute(parts[d], "red", ring_z(d)) for d in (1, 2, 3)]
    terms = pl.pallas_call(
        sum_kernel,
        grid=(2,),
        out_shape=[jax.ShapeDtypeStruct((held, rows, LANES), F32)] * RING,
        in_specs=[pl.BlockSpec((RING, held // 2, rows, LANES), lambda n: (0, n, 0, 0))] * RING,
        out_specs=[pl.BlockSpec((held // 2, rows, LANES), lambda n: (n, 0, 0))] * RING,
        compiler_params=params,
        cost_estimate=cost(m_rows * 512, 3 << 20),
        name="sums",
    )(*sums)
    back = [terms[0]] + [lax.ppermute(terms[d], "blk", ring_y(RING - d)) for d in (1, 2, 3)]

    return pl.pallas_call(
        functools.partial(update_kernel, slots),
        grid=(n_i // 4,),
        out_shape=jax.ShapeDtypeStruct(integrals.shape, F32),
        in_specs=[SMEM] * 4
        + [row_spec] * 3
        + [whole((held, rows, LANES))] * RING
        + [pl.BlockSpec((4, n_j, rows, kept), lambda n: (n, 0, 0, 0))],
        out_specs=pl.BlockSpec((4, n_j, rows, kept), lambda n: (n, 0, 0, 0)),
        scratch_shapes=[
            pltpu.VMEM((3 * LANES, CORES * kept), BF16),
            pltpu.VMEM((rows, 1), I32),
            pltpu.VMEM((rows, 1), F32),
            pltpu.VMEM((n_i, RING * rows, 3 * LANES), BF16),
        ],
        compiler_params=params,
        cost_estimate=cost(2 * 3 * m_rows * 128 * 512, 4 << 20),
        name="update",
    )(occ_irrep, slab_i, slab_j, occ_energy, lv, ve, part, *back, integrals)


def on_device(
    amplitudes,
    dressed,
    integrals,
    occ_irrep,
    virt_irrep,
    occ_energy,
    virt_energy,
    slab_i,
    slab_j,
    slab_k,
):
    pb_y, rank, part, fits = pack_dressed(
        PARTS[1], dressed, occ_irrep, virt_irrep, slab_j, slab_k
    )
    pb_y = over_y(pb_y)
    pa = pack_amplitudes(WIDES[1], amplitudes, rank, occ_irrep, virt_irrep, slab_i, slab_k)
    rest = (integrals, occ_irrep, virt_irrep, occ_energy, virt_energy, slab_i, slab_j, slab_k)

    def dense(pb_y, pa, rank, part, fits, a, d, *rest):
        return dense_form(a, d, *rest)

    def loose(pb_y, pa, rank, part, fits, a, d, *rest):
        pb, rank, part, _ = pack_dressed(PARTS[0], d, rest[1], rest[2], rest[6], rest[7])
        pa = pack_amplitudes(WIDES[0], a, rank, rest[1], rest[2], rest[5], rest[7])
        return packed_form(PARTS[0], over_y(pb), pa, rank, part, a, *rest)

    def tight(pb_y, pa, rank, part, fits, a, d, *rest):
        return packed_form(PARTS[1], pb_y, pa, rank, part, a, *rest)

    def other(pb_y, pa, rank, part, fits, *arrays):
        return lax.cond(fits[0] == 1, loose, dense, pb_y, pa, rank, part, fits, *arrays)

    return lax.cond(
        fits[0] == 2, tight, other, pb_y, pa, rank, part, fits, amplitudes, dressed, *rest
    )


def solution(mesh):
    in_specs = (
        P("red", None, "blk", None),
        P("red", None, "blk", None),
        P(None, None, "blk", "red"),
        P(),
        P(),
        P(),
        P(),
        P(),
        P(),
        P("red"),
    )
    out_specs = P(None, None, "blk", "red")
    return jax.shard_map(
        on_device, mesh=mesh, in_specs=in_specs, out_specs=out_specs, check_vma=False
    )
```

```python
import functools

import jax
import jax.numpy as jnp
import numpy as np
from jax import lax
from jax.experimental import pallas as pl
from jax.experimental.pallas import tpu as pltpu
from jax.sharding import PartitionSpec as P

F32 = jnp.float32
BF16 = jnp.bfloat16
I32 = jnp.int32

RING = 4
CORES = 2
WIDES = (192, 160)
PARTS = (64, 48)
STEPS = (1, 3, 2, 0)
LANES = 128


def table_lookup(table, picks):
    hits = picks[:, None] == jnp.arange(table.shape[0], dtype=jnp.int32)[None, :]
    return jnp.sum(jnp.where(hits, table[None, :], jnp.zeros((), table.dtype)), axis=1)


def dense_form(
    amplitudes,
    dressed,
    integrals,
    occ_irrep,
    virt_irrep,
    occ_energy,
    virt_energy,
    slab_i,
    slab_j,
    slab_k,
):
    blk_size = lax.axis_size("blk")
    red_size = lax.axis_size("red")
    k_local, slab_rows, virt_rows, virt_all = amplitudes.shape
    occ_cols = dressed.shape[1]
    cols_kept = virt_all // red_size
    pair_count = slab_rows * occ_cols // blk_size
    own_rows = max(1, pair_count // occ_cols)
    own_cols = min(pair_count, occ_cols)
    owners = np.arange(blk_size)
    first_pair = owners * pair_count
    table_rows = ((first_pair // occ_cols)[:, None] + np.arange(own_rows)[None, :]).reshape(-1)
    table_cols = ((first_pair % occ_cols)[:, None] + np.arange(own_cols)[None, :]).reshape(-1)
    blk_place = lax.axis_index("blk")
    red_place = lax.axis_index("red")
    label_i = table_lookup(occ_irrep, slab_i)
    label_j = table_lookup(occ_irrep, slab_j)
    label_k = table_lookup(occ_irrep, slab_k)
    rows_label = lax.dynamic_slice_in_dim(virt_irrep, blk_place * virt_rows, virt_rows)
    pair_virt = jnp.bitwise_xor(rows_label[:, None], virt_irrep[None, :])
    amp_sym = jnp.bitwise_xor(
        jnp.bitwise_xor(label_k[:, None], label_i[None, :])[:, :, None, None], pair_virt[None, None]
    )
    kept_amp = jnp.where(amp_sym == 0, amplitudes, jnp.zeros((), amplitudes.dtype))
    dre_sym = jnp.bitwise_xor(
        jnp.bitwise_xor(label_k[:, None], label_j[None, :])[:, :, None, None], pair_virt[None, None]
    )
    kept_dre = jnp.where(dre_sym == 0, dressed, jnp.zeros((), dressed.dtype))
    send_amp = jnp.take(kept_amp, table_rows, axis=1).reshape(
        k_local, blk_size, own_rows, virt_rows, virt_all
    )
    send_dre = jnp.take(kept_dre, table_cols, axis=1).reshape(
        k_local, blk_size, own_cols, virt_rows, virt_all
    )
    amp_owner = lax.all_to_all(send_amp, "blk", split_axis=1, concat_axis=3, tiled=True)[:, 0]
    dre_owner = lax.all_to_all(send_dre, "blk", split_axis=1, concat_axis=3, tiled=True)[:, 0]
    partial_cycle = jnp.einsum(
        "kiac,kjcb->ijab", amp_owner, dre_owner, preferred_element_type=jnp.float32
    )
    by_cols = partial_cycle.reshape(pair_count, virt_all, red_size, cols_kept)
    cycle_pairs = lax.all_to_all(by_cols, "red", split_axis=2, concat_axis=2, tiled=True).sum(axis=2)
    cycle_kept = lax.all_to_all(
        cycle_pairs, "blk", split_axis=1, concat_axis=0, tiled=True
    ).reshape(slab_rows, occ_cols, virt_rows, cols_kept)
    energy_i = table_lookup(occ_energy, slab_i)
    energy_j = table_lookup(occ_energy, slab_j)
    energy_a = lax.dynamic_slice_in_dim(virt_energy, blk_place * virt_rows, virt_rows)
    energy_b = lax.dynamic_slice_in_dim(virt_energy, red_place * cols_kept, cols_kept)
    label_b = lax.dynamic_slice_in_dim(virt_irrep, red_place * cols_kept, cols_kept)
    denom = (
        energy_i[:, None, None, None]
        + energy_j[None, :, None, None]
        - energy_a[None, None, :, None]
        - energy_b[None, None, None, :]
    )
    out_virt = jnp.bitwise_xor(rows_label[:, None], label_b[None, :])
    out_sym = jnp.bitwise_xor(
        jnp.bitwise_xor(label_i[:, None], label_j[None, :])[:, :, None, None], out_virt[None, None]
    )
    value = (integrals.astype(jnp.float32) + cycle_kept) / denom
    return jnp.where(out_sym == 0, value, jnp.zeros((), jnp.float32))


def coords():
    blk = lax.axis_index("blk")
    return blk // (RING * CORES), (blk // CORES) % RING, blk % CORES, lax.axis_index("red")


def iota(shape, dim):
    return lax.broadcasted_iota(I32, shape, dim)


def picked_column(row, first, count):
    wide = row.shape[1]
    hit = iota((count, wide), 1) == iota((count, wide), 0) + first
    kept = jnp.where(hit, jnp.broadcast_to(row.astype(F32), (count, wide)), 0.0)
    return jnp.sum(kept, axis=1, keepdims=True).astype(row.dtype)


def one_hot(count, first, row):
    slot = (iota((count, 1), 0) + first).astype(F32).astype(BF16)
    there = jnp.clip(row, -1, 256).astype(F32).astype(BF16)
    return jnp.where(slot == there, jnp.ones((), BF16), jnp.zeros((), BF16))


def rest_hot(groups, group, half, rank):
    share = half // groups
    slot = iota((half, 1), 0) - group * share
    inside = jnp.logical_and(slot >= 0, slot < share)
    slot = jnp.where(inside, slot + half, 512).astype(F32).astype(BF16)
    there = jnp.clip(rank, -1, 256).astype(F32).astype(BF16)
    return jnp.where(slot == there, jnp.ones((), BF16), jnp.zeros((), BF16))


def label_ranks(lv_ref, rank_ref, part_ref, fits_ref):
    wide = lv_ref.shape[1]
    quarter = wide // RING
    tri = (iota((quarter, quarter), 0) < iota((quarter, quarter), 1)).astype(F32).astype(BF16)
    base = jnp.zeros((16, 1), F32)
    most_part = jnp.zeros((1, 1), F32)
    for part in range(RING):
        lanes = slice(part * quarter, (part + 1) * quarter)
        member = (iota((16, quarter), 0) == lv_ref[:, lanes]).astype(F32)
        before = jnp.dot(member.astype(BF16), tri, preferred_element_type=F32)
        part_ref[:, lanes] = jnp.sum(member * before, axis=0, keepdims=True).astype(I32)
        rank_ref[:, lanes] = jnp.sum(member * (before + base), axis=0, keepdims=True).astype(I32)
        count = jnp.sum(member, axis=1, keepdims=True)
        most_part = jnp.maximum(most_part, jnp.max(count))
        base = base + count
    most = jnp.max(most_part)
    whole_most = jnp.max(base)
    fits = jnp.logical_and(whole_most <= WIDES[0], most <= PARTS[0])
    tight = jnp.logical_and(whole_most <= WIDES[1], most <= PARTS[1])
    fits_ref[0] = fits.astype(I32) + tight.astype(I32)


def masked_rows(kept, at, label, own_label, lv, block):
    rows = block.shape[0]
    wanted = jnp.bitwise_xor(own_label, label).astype(F32).astype(BF16)
    kept[at * rows : (at + 1) * rows, :] = jnp.where(wanted == lv, block, jnp.zeros((), BF16))


def pack_dressed_kernel(
    slots,
    occ_ref,
    sj_ref,
    sk_ref,
    lv_ref,
    dre_ref,
    p0,
    p1,
    p2,
    p3,
    rank_ref,
    part_ref,
    fits_ref,
    hot_part,
    own_label,
    kept,
):
    _, y, _, z = coords()
    n = pl.program_id(0)
    n_k, _, rows, wide = dre_ref.shape
    lv = lv_ref[...].astype(F32).astype(BF16)

    @pl.when(n == 0)
    def _():
        label_ranks(lv_ref, rank_ref, part_ref, fits_ref)
        step = (iota((1, wide), 1) // (wide // RING) - z + RING) % RING
        first = jnp.zeros((1, wide), I32)
        for n_step, s in enumerate(STEPS):
            first = jnp.where(step == s, n_step * slots, first)
        place = first + jnp.minimum(part_ref[...], slots - 1)
        hot_part[...] = one_hot(RING * slots, 0, place).T
        own_label[...] = picked_column(lv_ref[...], lax.axis_index("blk") * rows, rows)

    for k in range(n_k):
        lk = occ_ref[sk_ref[n * n_k + k]]
        for d in range(RING):
            for jj in range(CORES):
                j = ((y + d) % RING) * CORES + jj
                label = jnp.bitwise_xor(lk, occ_ref[sj_ref[j]])
                at = (jj * RING + d) * n_k + k
                masked_rows(kept, at, label, own_label[...], lv, dre_ref[k, j])
    count = n_k * rows
    packed = jnp.dot(kept[...], hot_part[...], preferred_element_type=F32)
    for d, out in enumerate((p0, p1, p2, p3)):
        even = packed[d * count : (d + 1) * count]
        odd = packed[(RING + d) * count : (RING + d + 1) * count]
        pieces = []
        for s in range(RING):
            at = slice(s * slots, (s + 1) * slots)
            pieces += [even[:, at], odd[:, at]]
        out[...] = jnp.concatenate(pieces, axis=1).astype(BF16).reshape(out.shape)


def pack_amplitudes_kernel(
    occ_ref,
    si_ref,
    sk_ref,
    lv_ref,
    rank_ref,
    amp_ref,
    pa_ref,
    hot_main,
    hot_rest,
    own_label,
    kept,
):
    n = pl.program_id(0)
    n_k, n_i, rows, wide = amp_ref.shape
    half = hot_main.shape[1]
    groups = hot_rest.shape[0]
    lv = lv_ref[...].astype(F32).astype(BF16)

    @pl.when(n == 0)
    def _():
        rank = rank_ref[...]
        hot_main[...] = one_hot(half, 0, rank).T
        for group in range(groups):
            hot_rest[group] = rest_hot(groups, group, half, rank).T
        own_label[...] = picked_column(lv_ref[...], lax.axis_index("blk") * rows, rows)

    for i in range(n_i):
        for k in range(n_k):
            label = jnp.bitwise_xor(occ_ref[sk_ref[n * n_k + k]], occ_ref[si_ref[i]])
            masked_rows(kept, i * n_k + k, label, own_label[...], lv, amp_ref[k, i])
    main = jnp.dot(kept[...], hot_main[...], preferred_element_type=F32).astype(BF16)
    count = n_i * n_k * rows // groups
    rest = jnp.zeros((count, half), F32)
    for group in range(groups):
        block = kept[group * count : (group + 1) * count]
        rest += jnp.dot(block, hot_rest[group], preferred_element_type=F32)
    main = main.reshape(n_i, n_k, rows, half)
    rest = rest.astype(BF16).reshape(n_i // groups, n_k, rows, half)
    for d in range(RING):
        for k in range(n_k):
            pa_ref[d, k, :n_i] = main[:, k]
            pa_ref[d, k, n_i:] = rest[:, k]


def unpack_kernel(
    occ_ref, si_ref, sk_ref, lv_ref, rank_ref, pa_ref, out_ref, hot, order, labels
):
    x, y, core, _ = coords()
    k = pl.program_id(0)
    n_rest, rows, half = pa_ref.shape[2:]
    groups = hot.shape[0]
    n_i = n_rest * groups // (groups + 1)
    wide = lv_ref.shape[1]

    @pl.when(k == 0)
    def _():
        p = iota((1, wide), 1)
        source = (
            ((x - (p // (4 * rows)) % RING + RING) % RING) * (rows * 8)
            + ((y - (p // rows) % RING + RING) % RING) * (rows * 2)
            + jnp.bitwise_xor(core, p // (wide // 2)) * rows
            + p % rows
        )
        pick = (iota((wide, wide), 0) == source).astype(F32).astype(BF16)
        which = iota((16, wide), 0)
        both = jnp.where(
            which == 0,
            jnp.broadcast_to(lv_ref[...], (16, wide)),
            jnp.broadcast_to(jnp.minimum(rank_ref[...], 255), (16, wide)),
        )
        moved = jnp.dot(both.astype(F32).astype(BF16), pick, preferred_element_type=F32).astype(I32)
        order[...] = moved[0:1].astype(F32).astype(BF16)
        rank = moved[1:2]
        main = one_hot(half, 0, rank)
        for side in range(groups):
            hot[side, :half] = main
            hot[side, half:] = rest_hot(groups, side, half, rank)
        for d in range(RING):
            first = x * (rows * 8) + ((y - d + RING) % RING) * (rows * 2) + core * rows
            labels[d] = picked_column(lv_ref[...], first, rows)

    for e in range(out_ref.shape[0]):
        lk = occ_ref[sk_ref[k * out_ref.shape[0] + e]]
        group = n_i // groups
        blocks = [pa_ref.at[(y - d + RING) % RING] for d in range(RING)]
        for side in range(groups):
            pairs = []
            for block in blocks:
                main = block[e, side * group : (side + 1) * group].reshape(group * rows, half)
                rest = block[e, n_i:].reshape(group * rows, half)
                pairs.append(jnp.concatenate([main, rest], axis=1))
            spread = jnp.dot(
                jnp.concatenate(pairs, axis=0), hot[side], preferred_element_type=F32
            )
            for d in range(RING):
                for g in range(group):
                    i = side * group + g
                    label = jnp.bitwise_xor(lk, occ_ref[si_ref[i]])
                    wanted = jnp.bitwise_xor(labels[d], label).astype(F32).astype(BF16)
                    at = (d * n_i + i) * rows
                    source = (d * group + g) * rows
                    out_ref[e, at : at + rows, :] = jnp.where(
                        wanted == order[...],
                        spread[source : source + rows].astype(BF16),
                        jnp.zeros((), BF16),
                    )


def folded(value, n_i, rows):
    used = value.shape[1]
    blocks = [value[n * rows : (n + 1) * rows] for n in range(value.shape[0] // rows)]
    if used == LANES:
        return blocks
    hosts = used // (LANES - used)
    held = n_i * hosts // (hosts + 1)
    out = []
    for d in range(len(blocks) // n_i):
        for i in range(held):
            guest = blocks[d * n_i + held + i // hosts]
            at = (i % hosts) * (LANES - used)
            out.append(
                jnp.concatenate([blocks[d * n_i + i], guest[:, at : at + LANES - used]], axis=1)
            )
    return out


def cycle_kernel(
    n_i, slots, first, a_ref, b0, b1, b2, b3, b4, b5, b6, b7, o0, o1, b_all, total
):
    k = pl.program_id(0)
    rows = b0.shape[2]
    depth = b0.shape[0] * rows
    start = first * CORES * slots // LANES * LANES
    term = None
    for e in range(a_ref.shape[0]):
        for n, b in enumerate((b0, b1, b2, b3, b4, b5, b6, b7)):
            block = b[:, e, :, start : start + 256].reshape(depth, 256)
            b_all[e, n * depth : (n + 1) * depth, :] = block
        part = jnp.dot(a_ref[e], b_all[e], preferred_element_type=F32)
        term = part if term is None else term + part

    @pl.when(k == 0)
    def _():
        total[...] = term

    @pl.when(jnp.logical_and(k > 0, k < pl.num_programs(0) - 1))
    def _():
        total[...] += term

    @pl.when(k == pl.num_programs(0) - 1)
    def _():
        full = total[...] + term
        for n, out in enumerate((o0, o1)):
            at = (first + n) * CORES * slots - start
            for m, block in enumerate(folded(full[:, at : at + CORES * slots], n_i, rows)):
                out[m // out.shape[1], m % out.shape[1]] = block


def sum_kernel(o0, o1, o2, o3, s0, s1, s2, s3):
    for d, out in enumerate((s0, s1, s2, s3)):
        out[...] = ((o0[d] + o1[d]) + o2[d]) + o3[d]


def update_kernel(
    slots,
    occ_ref,
    si_ref,
    sj_ref,
    oe_ref,
    lv_ref,
    ve_ref,
    part_ref,
    t0,
    t1,
    t2,
    t3,
    int_ref,
    out_ref,
    hot,
    own_label,
    own_energy,
    three,
):
    _, y, _, z = coords()
    n = pl.program_id(0)
    held, rows, lanes = t0.shape
    n_i, _, _, kept = int_ref.shape
    cols = pl.ds(pl.multiple_of(z * kept, kept), kept)

    @pl.when(n == 0)
    def _():
        slot = iota((lanes, kept), 0)
        part = part_ref[:, cols]
        for jj in range(CORES):
            one = (slot == part + jj * slots).astype(F32).astype(BF16)
            for n in range(3):
                hot[n * lanes : (n + 1) * lanes, jj * kept : (jj + 1) * kept] = one
        first = lax.axis_index("blk") * rows
        own_label[...] = picked_column(lv_ref[...], first, rows)
        own_energy[...] = picked_column(ve_ref[...], first, rows)

    spare = lanes - CORES * slots

    @pl.when(n == 0)
    def _():
        for d, t in enumerate((t0, t1, t2, t3)):
            for i in range(three.shape[0]):
                if i < held:
                    x = t[i]
                else:
                    hosts = CORES * slots // spare
                    first_host = (i - held) * hosts
                    x = jnp.concatenate(
                        [t[first_host + h][:, lanes - spare :] for h in range(hosts)]
                        + [jnp.zeros((rows, spare), F32)],
                        axis=1,
                    )
                top = x.astype(BF16)
                left = x - top.astype(F32)
                mid = left.astype(BF16)
                low = (left - mid.astype(F32)).astype(BF16)
                three[i, d * rows : (d + 1) * rows] = jnp.concatenate([top, mid, low], axis=1)

    label_b = lv_ref[:, cols]
    energy_b = ve_ref[:, cols]
    for e in range(n_i):
        i = n * n_i + e
        cycle = jnp.dot(three[i], hot[...], preferred_element_type=F32)
        label_i = occ_ref[si_ref[i]]
        energy_i = oe_ref[si_ref[i]]
        for d in range(RING):
            for jj in range(CORES):
                j = ((y + d) % RING) * CORES + jj
                label = jnp.bitwise_xor(label_i, occ_ref[sj_ref[j]])
                denom = ((energy_i + oe_ref[sj_ref[j]]) - own_energy[...]) - energy_b
                term = cycle[d * rows : (d + 1) * rows, jj * kept : (jj + 1) * kept]
                value = (int_ref[e, j].astype(F32) + term) / denom
                keep = jnp.bitwise_xor(own_label[...], label) == label_b
                out_ref[e, j] = jnp.where(keep, value, 0.0)


SMEM = pl.BlockSpec(memory_space=pltpu.SMEM)


def whole(shape):
    return pl.BlockSpec(shape, lambda n: (0,) * len(shape))


def cost(flops, moved):
    return pl.CostEstimate(flops=flops, bytes_accessed=moved, transcendentals=0)


def halves(shape, dim):
    block = tuple(size // 2 if at == dim else size for at, size in enumerate(shape))
    return pl.BlockSpec(block, lambda n: tuple(n if at == dim else 0 for at in range(len(shape))))


def pack_dressed(slots, dressed, occ_irrep, virt_irrep, slab_j, slab_k):
    n_k, n_j, rows, wide = dressed.shape
    out = (n_k, rows, RING * CORES * slots)
    row_spec = whole((1, wide))
    row = jax.ShapeDtypeStruct((1, wide), I32)
    *pb, rank, part, fits = pl.pallas_call(
        functools.partial(pack_dressed_kernel, slots),
        grid=(2,),
        out_shape=[jax.ShapeDtypeStruct(out, BF16)] * RING
        + [row, row, jax.ShapeDtypeStruct((1,), I32)],
        in_specs=[SMEM] * 3 + [row_spec, halves(dressed.shape, 0)],
        out_specs=[halves(out, 0)] * RING + [row_spec, row_spec, SMEM],
        scratch_shapes=[
            pltpu.VMEM((wide, RING * slots), BF16),
            pltpu.VMEM((rows, 1), I32),
            pltpu.VMEM((n_k * n_j * rows // 2, wide), BF16),
        ],
        compiler_params=pltpu.CompilerParams(vmem_limit_bytes=32 * 1024 * 1024),
        cost_estimate=cost(2 * n_k * n_j * rows * wide * 256, 10 << 20),
        name="pack_dressed",
    )(occ_irrep, slab_j, slab_k, virt_irrep.reshape(1, wide), dressed)
    return pb, rank, part, fits


def pack_amplitudes(slots, amplitudes, rank, occ_irrep, virt_irrep, slab_i, slab_k):
    n_k, n_i, rows, wide = amplitudes.shape
    half = LANES
    groups = half // (slots - half)
    out = (RING, n_k, n_i + n_i // groups, rows, half)
    row_spec = whole((1, wide))
    return pl.pallas_call(
        pack_amplitudes_kernel,
        grid=(2,),
        out_shape=jax.ShapeDtypeStruct(out, BF16),
        in_specs=[SMEM] * 3 + [row_spec, row_spec, halves(amplitudes.shape, 0)],
        out_specs=halves(out, 1),
        scratch_shapes=[
            pltpu.VMEM((wide, half), BF16),
            pltpu.VMEM((groups, wide, half), BF16),
            pltpu.VMEM((rows, 1), I32),
            pltpu.VMEM((n_k * n_i * rows // 2, wide), BF16),
        ],
        compiler_params=pltpu.CompilerParams(vmem_limit_bytes=32 * 1024 * 1024),
        cost_estimate=cost(2 * n_k * n_i * rows * wide * 256, 10 << 20),
        name="pack_amplitudes",
    )(occ_irrep, slab_i, slab_k, virt_irrep.reshape(1, wide), rank, amplitudes)


def ring_y(d):
    return [
        (8 * x + 2 * y + c, 8 * x + 2 * ((y + d) % RING) + c)
        for x in range(RING)
        for y in range(RING)
        for c in range(CORES)
    ]


def groups_y():
    return [
        [8 * x + 2 * y + c for y in range(RING)] for x in range(RING) for c in range(CORES)
    ]


def ring_x(d):
    return [
        (8 * x + m, 8 * ((x + d) % RING) + m) for x in range(RING) for m in range(RING * CORES)
    ]


def ring_z(d):
    return [(z, (z + d) % RING) for z in range(RING)]


def other_core():
    return [(b, b ^ 1) for b in range(RING * RING * CORES)]


def over_y(pb):
    return jnp.stack([pb[0]] + [lax.ppermute(pb[d], "blk", ring_y(d)) for d in (1, 2, 3)])


def packed_form(
    slots,
    pb_y,
    pa,
    rank,
    part,
    amplitudes,
    integrals,
    occ_irrep,
    virt_irrep,
    occ_energy,
    virt_energy,
    slab_i,
    slab_j,
    slab_k,
):
    n_k, n_i, rows, wide = amplitudes.shape
    n_j = integrals.shape[1]
    kept = integrals.shape[3]
    half = LANES
    n_rest = pa.shape[2]
    groups = n_i // (n_rest - n_i)
    n_cols = RING * CORES * slots
    held = n_i * CORES * slots // LANES
    lv = virt_irrep.reshape(1, wide)
    ve = virt_energy.reshape(1, wide)
    row_spec = whole((1, wide))
    params = pltpu.CompilerParams(vmem_limit_bytes=32 * 1024 * 1024)

    pa_y = lax.all_to_all(pa, "blk", 0, 0, axis_index_groups=groups_y())

    m_rows = RING * n_i * rows
    spread = pl.pallas_call(
        unpack_kernel,
        grid=(n_k // 2,),
        out_shape=jax.ShapeDtypeStruct((n_k, m_rows, wide), BF16),
        in_specs=[SMEM] * 3
        + [row_spec] * 2
        + [pl.BlockSpec((RING, 2, n_rest, rows, half), lambda k: (0, k, 0, 0, 0))],
        out_specs=pl.BlockSpec((2, m_rows, wide), lambda k: (k, 0, 0)),
        scratch_shapes=[
            pltpu.VMEM((groups, 2 * half, wide), BF16),
            pltpu.VMEM((1, wide), BF16),
            pltpu.VMEM((RING, rows, 1), I32),
        ],
        compiler_params=params,
        cost_estimate=cost(2 * n_k * m_rows * wide * 256, 20 << 20),
        name="unpack",
    )(occ_irrep, slab_i, slab_k, lv, rank, pa_y)

    mine = pb_y
    across = [mine] + [lax.ppermute(mine, "blk", ring_x(d)) for d in (1, 2, 3)]
    *across[2:], spread = lax.optimization_barrier((*across[2:], spread))
    twin = [lax.ppermute(b, "blk", other_core()) for b in across]
    parts = {}
    for first in (0, 2):
        parts[STEPS[first]], parts[STEPS[first + 1]] = pl.pallas_call(
            functools.partial(cycle_kernel, n_i, slots, first),
            grid=(n_k // 2,),
            out_shape=[jax.ShapeDtypeStruct((RING, held, rows, LANES), F32)] * 2,
            in_specs=[pl.BlockSpec((2, m_rows, wide), lambda k: (k, 0, 0))]
            + [pl.BlockSpec((RING, 2, rows, n_cols), lambda k: (0, k, 0, 0))] * 8,
            out_specs=[whole((RING, held, rows, LANES))] * 2,
            scratch_shapes=[pltpu.VMEM((2, wide, 256), BF16), pltpu.VMEM((m_rows, 256), F32)],
            compiler_params=params,
            cost_estimate=cost(2 * n_k * m_rows * wide * 256, 14 << 20),
            name="cycle",
        )(spread, *across, *twin)

    sums = [parts[0]] + [lax.ppermute(parts[d], "red", ring_z(d)) for d in (1, 2, 3)]
    terms = pl.pallas_call(
        sum_kernel,
        grid=(2,),
        out_shape=[jax.ShapeDtypeStruct((held, rows, LANES), F32)] * RING,
        in_specs=[pl.BlockSpec((RING, held // 2, rows, LANES), lambda n: (0, n, 0, 0))] * RING,
        out_specs=[pl.BlockSpec((held // 2, rows, LANES), lambda n: (n, 0, 0))] * RING,
        compiler_params=params,
        cost_estimate=cost(m_rows * 512, 3 << 20),
        name="sums",
    )(*sums)
    back = [terms[0]] + [lax.ppermute(terms[d], "blk", ring_y(RING - d)) for d in (1, 2, 3)]

    return pl.pallas_call(
        functools.partial(update_kernel, slots),
        grid=(n_i // 4,),
        out_shape=jax.ShapeDtypeStruct(integrals.shape, F32),
        in_specs=[SMEM] * 4
        + [row_spec] * 3
        + [whole((held, rows, LANES))] * RING
        + [pl.BlockSpec((4, n_j, rows, kept), lambda n: (n, 0, 0, 0))],
        out_specs=pl.BlockSpec((4, n_j, rows, kept), lambda n: (n, 0, 0, 0)),
        scratch_shapes=[
            pltpu.VMEM((3 * LANES, CORES * kept), BF16),
            pltpu.VMEM((rows, 1), I32),
            pltpu.VMEM((rows, 1), F32),
            pltpu.VMEM((n_i, RING * rows, 3 * LANES), BF16),
        ],
        compiler_params=params,
        cost_estimate=cost(2 * 3 * m_rows * 128 * 512, 4 << 20),
        name="update",
    )(occ_irrep, slab_i, slab_j, occ_energy, lv, ve, part, *back, integrals)


def on_device(
    amplitudes,
    dressed,
    integrals,
    occ_irrep,
    virt_irrep,
    occ_energy,
    virt_energy,
    slab_i,
    slab_j,
    slab_k,
):
    pb_y, rank, part, fits = pack_dressed(
        PARTS[1], dressed, occ_irrep, virt_irrep, slab_j, slab_k
    )
    pb_y = over_y(pb_y)
    pa = pack_amplitudes(WIDES[1], amplitudes, rank, occ_irrep, virt_irrep, slab_i, slab_k)
    rest = (integrals, occ_irrep, virt_irrep, occ_energy, virt_energy, slab_i, slab_j, slab_k)

    def dense(pb_y, pa, rank, part, fits, a, d, *rest):
        return dense_form(a, d, *rest)

    def loose(pb_y, pa, rank, part, fits, a, d, *rest):
        pb, rank, part, _ = pack_dressed(PARTS[0], d, rest[1], rest[2], rest[6], rest[7])
        pa = pack_amplitudes(WIDES[0], a, rank, rest[1], rest[2], rest[5], rest[7])
        return packed_form(PARTS[0], over_y(pb), pa, rank, part, a, *rest)

    def tight(pb_y, pa, rank, part, fits, a, d, *rest):
        return packed_form(PARTS[1], pb_y, pa, rank, part, a, *rest)

    def other(pb_y, pa, rank, part, fits, *arrays):
        return lax.cond(fits[0] == 1, loose, dense, pb_y, pa, rank, part, fits, *arrays)

    return lax.cond(
        fits[0] == 2, tight, other, pb_y, pa, rank, part, fits, amplitudes, dressed, *rest
    )


def solution(mesh):
    in_specs = (
        P("red", None, "blk", None),
        P("red", None, "blk", None),
        P(None, None, "blk", "red"),
        P(),
        P(),
        P(),
        P(),
        P(),
        P(),
        P("red"),
    )
    out_specs = P(None, None, "blk", "red")
    return jax.shard_map(
        on_device, mesh=mesh, in_specs=in_specs, out_specs=out_specs, check_vma=False
    )
```
